256 devices in a mesh: ex: 16 (over y, x), par: 16 (over z, core).
Axes of the slice: x: 4, y: 4, z: 8, core: 2. Of those that a mesh axis runs over, the one named last changes fastest.
Arguments:
- adapter_inputs: bfloat16 [384, 256, 64], P('ex'), may hold values from -6 to 6
- output_gradient: bfloat16 [384, 256, 4096], P('ex', None, 'par'), may hold values from -0.29882812 to 0.29882812
- lengths: int32 [384], P('ex'), may hold values from 1 to 256, 61440 in all
- projection: bfloat16 [262144, 4096], P(('par', 'ex')), may hold values from -1 to 1
- validation_feature_rows: bfloat16 [4096, 4096], P('par', 'ex'), may hold values from -6 to 6
Outputs:
- features: bfloat16 [384, 4096], P('par', 'ex')
- scores: float32 [384, 4096], P('par', 'ex')
The draws below stay inside these ranges and needn't reach their ends.
Inputs may be any that keep to these rules, and one draw needn't show every extreme that they name: `lengths`: each example's number of live tokens; its later positions are padding. The largest is 256.
All inputs are finite; a program needn't handle non-finite values. No bound on the sum of `lengths` on one device may be relied on, other than what follows from the above.
Results may differ from the reference program's by a relative error of at most 0.0051.
Values may be sent and summed in bfloat16 or wider, within the bound.
A program may use at most 64 MiB of HBM per device.

```python
import math
import jax
import jax.numpy as jnp
import numpy as np
from jax import lax

D = 4096
ADAPTER_RANK = 64
PROJ = 4096
VALID = 4096
TOKEN_LIMIT = 256
TRAIN_EXAMPLES = 384


def draw_projection(key, part):
    key = jax.random.fold_in(key, 11)
    noise_key, row_key, column_key = jax.random.split(key, 3)
    param_rows = ADAPTER_RANK * D
    noise = jax.random.truncated_normal(noise_key, -4.0, 4.0, (param_rows, PROJ), jnp.float32)
    share = 0.7
    row_factor = jax.random.truncated_normal(row_key, -4.0, 4.0, (param_rows, 1), jnp.float32)
    common = jax.random.truncated_normal(column_key, -4.0, 4.0, (1, PROJ), jnp.float32)
    scale = (1.0 / (1.0 + share * share)) ** 0.5 * float(param_rows) ** (-0.5)
    value = (noise + share * row_factor * common) * scale
    return value.astype(jnp.bfloat16)


def shard_levels(stream_key, dims, cuts, smallest, high):
    def one(dim, shards_of):
        steps = jax.random.uniform(jax.random.fold_in(jax.random.fold_in(stream_key, 6), dim), (shards_of,), jnp.float32, smallest / len(cuts), high / len(cuts))
        return jnp.repeat(jnp.exp(steps), dims[dim] // shards_of).reshape((-1,) + (1,) * (len(dims) - dim - 1))

    loudness = one(*cuts[0])
    for cut in cuts[1:]:
        loudness = loudness * one(*cut)
    return loudness


def length_profile(amount, total, bound, slope):
    loads = [(1 << 20) // math.isqrt(standing ** slope) + 1 for standing in range(2, amount + 1)]
    surplus, counts = total - bound - (amount - 1), [1] * (amount - 1)
    while surplus > 0:
        candidates = [i for i in range(amount - 1) if counts[i] < bound]
        whole, remaining = sum([loads[i] for i in candidates]), surplus
        for i in candidates:
            addition = min(bound - counts[i], max(1, remaining * loads[i] // whole), surplus)
            counts[i] = counts[i] + addition
            surplus = surplus - addition
    return np.array([bound] + counts)


def uneven(own_key, amount, total, most, lean):
    if amount == 2:
        one = jax.random.randint(own_key, (), max(1, total - most), min(most, total - 1) + 1)
        return jnp.stack([one, total - one])
    tallies = jnp.asarray(length_profile(amount, total, most, lean), jnp.int32)
    twos = (amount - 1) // 2
    giver, sink = tallies[1:1 + 2 * twos:2], tallies[2:2 + 2 * twos:2]
    margin = jnp.minimum(giver - 1, most - sink)
    passed = jax.random.randint(jax.random.fold_in(own_key, 1), (twos,), 0, 1 << 20) % (margin + 1)
    tallies = tallies.at[1:1 + 2 * twos:2].set(giver - passed).at[2:2 + 2 * twos:2].set(sink + passed)
    return tallies[jax.random.permutation(jax.random.fold_in(own_key, 2), amount)]


def gaussian(own_key, shape, deviation, most, shards=(), kind=jnp.bfloat16):
    loudness = shard_levels(own_key, shape, shards, -0.22, 0.18) if shards else 1.0
    result = jax.random.normal(own_key, shape, jnp.float32) * deviation * loudness
    return jnp.minimum(jnp.maximum(result, -most), most).astype(kind)


def setup_inputs(seed: int = 0) -> dict:
    seeds = jax.random.split(jax.random.key(seed), 6)
    adapter_inputs = gaussian(seeds[0], (TRAIN_EXAMPLES, TOKEN_LIMIT, ADAPTER_RANK), 1.0, 6.0, ((0, 16),))
    output_gradient = gaussian(seeds[1], (TRAIN_EXAMPLES, TOKEN_LIMIT, D), 0.05, 0.29882812, ((0, 16), (2, 16)))
    lengths = uneven(seeds[2], TRAIN_EXAMPLES, TRAIN_EXAMPLES * TOKEN_LIMIT * 5 // 8, TOKEN_LIMIT, 0).astype(jnp.int32)
    projection = draw_projection(jax.random.fold_in(seeds[5], 71), 0)
    validation_feature_rows = gaussian(seeds[4], (VALID, PROJ), 1.0, 6.0, ((0, 16), (1, 16)))
    return dict(adapter_inputs=adapter_inputs, output_gradient=output_gradient, lengths=lengths, projection=projection, validation_feature_rows=validation_feature_rows)


def reference(adapter_inputs, output_gradient, lengths, projection, validation_feature_rows):

    def single_example(items):
        acts, grad_out, count = items
        live = jnp.arange(TOKEN_LIMIT, dtype=jnp.int32) < count
        masked_tokens = jnp.where(live[:, None], grad_out, jnp.zeros_like(grad_out))
        block = jnp.dot(masked_tokens.T, acts, preferred_element_type=jnp.float32)
        return block.astype(jnp.bfloat16).reshape(D * ADAPTER_RANK)
    example_gradients = lax.map(single_example, (adapter_inputs, output_gradient, lengths))
    projected = jnp.dot(example_gradients, projection, preferred_element_type=jnp.float32)
    features = projected.astype(jnp.bfloat16)
    wide = features.astype(jnp.float32)
    feat_sq = lax.optimization_barrier(jnp.sum(wide * wide, axis=1))
    val_wide = validation_feature_rows.astype(jnp.float32)
    val_sq = lax.optimization_barrier(jnp.sum(val_wide * val_wide, axis=1))
    dots = jnp.dot(features, validation_feature_rows.T, preferred_element_type=jnp.float32)
    factor = float(PROJ) ** 0.5
    scores = factor * dots * lax.rsqrt(feat_sq[:, None] + 1e-06) * lax.rsqrt(val_sq[None, :] + 1e-06)
    return (features, scores)
```

```python
import functools

import jax
import jax.numpy as jnp
from jax import lax
from jax.experimental import pallas as pl
from jax.experimental.pallas import tpu as pltpu
from jax.sharding import PartitionSpec as P

MESH = pl.DeviceIdType.MESH
F32 = jnp.float32
BF16 = jnp.bfloat16
LAG = 2


def kernel(
    ny, nx, nz, groups, rank,
    ai_hbm, og_hbm, len_ref, proj_hbm, val_hbm,
    feat_ref, score_ref,
    ai_v, og_v, proj_v, val_v, stage_v, send_a, recv_a, lhs, prod,
    send_c, recv_c, send_1, recv_1, keep_1, send_2, recv_2, keep_2,
    send_3, recv_3, val_sq, send_d, recv_d,
    ai_sem, og_sem, proj_sem, val_sem,
    as_sem, ar_sem, vs_sem, vr_sem, ws_sem, wr_sem, cs_sem, cr_sem,
    s1_sem, r1_sem, s2_sem, r2_sem, s3_sem, r3_sem, ds_sem, dr_sem,
):
    ex_n = ny * nx
    ex = lax.axis_index("ex")
    par = lax.axis_index("par")
    y, x = lax.div(ex, nx), lax.rem(ex, nx)
    z, core = lax.div(par, 2), lax.rem(par, 2)
    tokens = ai_v.shape[1]
    half_z = nz // 2

    def plane(oy, ox):
        return lax.rem(y + oy, ny) * nx + lax.rem(x + ox, nx)

    def depth(oz):
        return lax.rem(z + oz + nz, nz)

    def remote(src, dst, ssem, rsem, to_ex, to_par):
        return pltpu.make_async_remote_copy(
            src_ref=src, dst_ref=dst, send_sem=ssem, recv_sem=rsem,
            device_id=(to_ex, to_par), device_id_type=MESH,
        )

    for g in range(groups):
        rows = pl.ds(g * 8, 8)
        pltpu.make_async_copy(ai_hbm.at[rows], ai_v.at[rows], ai_sem.at[g]).start()
        pltpu.make_async_copy(og_hbm.at[rows], og_v.at[rows], og_sem.at[g]).start()
    val_copy = pltpu.make_async_copy(val_hbm, val_v.at[par], val_sem)
    val_copy.start()

    def proj_copy(s, q):
        return pltpu.make_async_copy(
            proj_hbm.at[pl.ds((q * 8 + s) * rank, rank)],
            proj_v.at[pl.ds(s * 2 * rank + q * rank, rank)],
            proj_sem.at[s, q],
        )

    for s in range(8):
        for q in range(2):
            proj_copy(s, q).start()

    barrier = pltpu.get_barrier_semaphore()

    def greet(to_ex, to_par):
        pl.semaphore_signal(barrier, inc=1, device_id=(to_ex, to_par), device_id_type=MESH)

    def greet_plane(o, _):
        greet(plane(lax.div(o, nx), lax.rem(o, nx)), par)
        return 0

    lax.fori_loop(1, ex_n, greet_plane, 0)

    def greet_depth(o, _):
        greet(ex, depth(o) * 2 + core)
        return 0

    lax.fori_loop(1, nz, greet_depth, 0)
    greet(ex, z * 2 + 1 - core)

    ring_plus, ring_minus = nz // 2, (nz - 1) // 2

    def val_hop(k, sign):
        slot = depth(-sign * (k - 1)) * 2 + core
        sem = k if sign > 0 else ring_plus + k
        return remote(
            val_v.at[slot], val_v.at[slot], vs_sem.at[sem], vr_sem.at[sem], ex, depth(sign) * 2 + core
        )

    def val_cross(k, sign):
        slot = depth(-sign * k) * 2 + core
        sem = k if sign > 0 else ring_plus + k
        return remote(
            val_v.at[slot], val_v.at[slot], ws_sem.at[sem], wr_sem.at[sem], ex, z * 2 + 1 - core
        )

    def val_point(k):
        if k == 0:
            val_copy.wait()
            val_cross(0, 1).start()
        else:
            if k <= ring_plus:
                val_hop(k, 1).wait_recv()
                val_cross(k, 1).start()
            if k <= ring_minus:
                val_hop(k, -1).wait_recv()
                val_cross(k, -1).start()
        if k + 1 <= ring_plus:
            val_hop(k + 1, 1).start()
        if k + 1 <= ring_minus:
            val_hop(k + 1, -1).start()

    lane = lax.broadcasted_iota(jnp.int32, (ex_n, 8, 128), 2)

    def a2a(g, o):
        to = plane(lax.div(o, nx), lax.rem(o, nx))
        return remote(
            send_a.at[g, to], recv_a.at[g, ex], as_sem.at[g, o], ar_sem.at[g, o], to, par
        )

    for g in range(groups):
        rows = pl.ds(g * 8, 8)
        pltpu.make_async_copy(ai_hbm.at[rows], ai_v.at[rows], ai_sem.at[g]).wait()
        pltpu.make_async_copy(og_hbm.at[rows], og_v.at[rows], og_sem.at[g]).wait()

        def gradient(e, _, g=g):
            m = g * 8 + e
            live = lax.broadcasted_iota(jnp.int32, (tokens, rank), 0) < len_ref[m]
            acts = jnp.where(live, ai_v[m].astype(F32), 0.0)
            acts = jnp.concatenate([acts, acts], axis=1).astype(BF16)
            out = lax.dot_general(
                og_v[m], acts, (((0,), (0,)), ((), ())), preferred_element_type=F32
            )
            out = out.reshape(ex_n, 2, 8, 2 * rank)
            both = jnp.where(lane < rank, out[:, 0], out[:, 1])
            stage_v[pl.ds(pl.multiple_of(e * ex_n * 8, ex_n * 8), ex_n * 8), :] = both.reshape(
                ex_n * 8, 2 * rank
            )
            return 0

        lax.fori_loop(0, 8, gradient, 0)

        def pack(j, _, g=g):
            for q in range(4):
                low = stage_v[pl.ds(j * 8 + q, 8, stride=ex_n * 8), :]
                high = stage_v[pl.ds(j * 8 + q + 4, 8, stride=ex_n * 8), :]
                send_a[g, j, :, q * 128 : (q + 1) * 128] = jnp.concatenate(
                    [low, high], axis=0
                ).astype(BF16)
            return 0

        lax.fori_loop(0, ex_n, pack, 0)
        recv_a[g, ex] = send_a[g, ex]
        if g == 0:
            pl.semaphore_wait(barrier, ex_n - 1 + nz - 1 + 1)

        def send(o, _, g=g):
            a2a(g, o).start()
            return 0

        lax.fori_loop(1, ex_n, send, 0)
        val_point(g)

    for g in range(groups):
        def arrive(o, _, g=g):
            a2a(g, o).wait_recv()
            return 0

        lax.fori_loop(1, ex_n, arrive, 0)

        def gather(t, _, g=g):
            pair = recv_a[g, pl.ds(2 * t, 2)].astype(F32)
            place = pl.ds(pl.multiple_of(g * ex_n * 8 + t * 16, 16), 16)
            for h in range(2):
                lhs[place, h * 512 : (h + 1) * 512] = jnp.concatenate(
                    [pair[0, h * 8 : h * 8 + 8], pair[1, h * 8 : h * 8 + 8]], axis=0
                ).astype(BF16)
            return 0

        lax.fori_loop(0, ex_n // 2, gather, 0)

    for k in range(groups, ring_plus + 1):
        val_point(k)
    for s in range(8):
        for q in range(2):
            proj_copy(s, q).wait()

    def offsets(t):
        return lax.rem(lax.div(t, nx) + 1, ny), lax.rem(lax.rem(t, nx) + 1, nx)

    def core_copy(t):
        return remote(
            send_c.at[t], recv_c.at[t], cs_sem.at[t], cr_sem.at[t], ex, z * 2 + 1 - core
        )

    def first_x(dy, dx):
        return remote(
            send_1.at[0, dx - 1, dy], recv_1.at[0, dx - 1, dy],
            s1_sem.at[0, dx - 1, dy], r1_sem.at[0, dx - 1, dy], plane(0, dx), par,
        )

    def first_y(dy, dx):
        return remote(
            send_1.at[1, dy - 1, dx], recv_1.at[1, dy - 1, dx],
            s1_sem.at[1, dy - 1, dx], r1_sem.at[1, dy - 1, dx], plane(dy, 0), par,
        )

    def pass_on(t):
        dy, dx = offsets(t)
        core_copy(t).wait_recv()
        slot = lax.rem(t, LAG + 1)

        def total(d):
            own = prod[slot, d, core].reshape(48, 128)
            return own + recv_c[t, d].astype(F32)

        @pl.when(dx == 0)
        def _():
            for d in range(half_z):
                keep_1[0, dy, d] = total(d)

        @pl.when(dx != 0)
        def _():
            for d in range(half_z):
                send_1[0, dx - 1, dy, d] = total(d).astype(BF16)
            first_x(dy, dx).start()

        @pl.when(dy == 0)
        def _():
            for d in range(half_z):
                keep_1[1, dx, d] = total(half_z + d)

        @pl.when(dy != 0)
        def _():
            for d in range(half_z):
                send_1[1, dy - 1, dx, d] = total(half_z + d).astype(BF16)
            first_y(dy, dx).start()

    def chunk(t, _):
        dy, dx = offsets(t)
        j = plane(dy, dx)
        out = jnp.dot(
            lhs[...], proj_v[:, pl.ds(pl.multiple_of(j * 256, 256), 256)],
            preferred_element_type=F32,
        )
        slot = lax.rem(t, LAG + 1)
        for l in range(2):
            for g in range(groups):
                prod[slot, :, :, l * groups + g] = out[
                    g * ex_n * 8 : (g + 1) * ex_n * 8, l * 128 : (l + 1) * 128
                ].reshape(nz, 2, 8, 128)
        for d in range(nz):
            send_c[t, d] = prod[slot, d, 1 - core].reshape(48, 128).astype(BF16)
        core_copy(t).start()

        @pl.when(t >= LAG)
        def _():
            pass_on(t - LAG)

        return 0

    lax.fori_loop(0, ex_n, chunk, 0)

    def rest(t, _):
        pass_on(t)
        return 0

    lax.fori_loop(ex_n - LAG, ex_n, rest, 0)

    for k in range(ring_plus + 1):
        val_cross(k, 1).wait_recv()
        if 1 <= k <= ring_minus:
            val_cross(k, -1).wait_recv()
    ones = jnp.ones((16, 256), BF16)

    def val_norm(b, _):
        wide = val_v[b].astype(F32)
        sq = wide * wide
        high = sq.astype(BF16)
        low = (sq - high.astype(F32)).astype(BF16)
        dims = (((1,), (1,)), ((), ()))
        val_sq[b] = (
            lax.dot_general(ones, high, dims, preferred_element_type=F32)
            + lax.dot_general(ones, low, dims, preferred_element_type=F32)
        )[0:8]
        return 0

    lax.fori_loop(0, val_v.shape[0], val_norm, 0)

    def second(part, o):
        to = plane(o, 0) if part == 0 else plane(0, o)
        return remote(
            send_2.at[part, o - 1], recv_2.at[part, o - 1],
            s2_sem.at[part, o - 1], r2_sem.at[part, o - 1], to, par,
        )

    for o in [*range(1, max(ny, nx)), 0]:
        for part in range(2):
            count, other = (ny, nx) if part == 0 else (nx, ny)
            if o >= count:
                continue
            for d in range(1, other):
                (first_x(o, d) if part == 0 else first_y(d, o)).wait_recv()
            for d in range(half_z):
                acc = keep_1[part, o, d]
                for i in range(other - 1):
                    acc += recv_1[part, i, o, d].astype(F32)
                if o == 0:
                    keep_2[part * half_z + d] = acc
                else:
                    send_2[part, o - 1, d] = acc.astype(BF16)
            if o != 0:
                second(part, o).start()

    def third(o):
        return remote(
            send_3.at[depth(o)], recv_3.at[o - 1], s3_sem.at[o - 1], r3_sem.at[o - 1],
            ex, depth(o) * 2 + core,
        )

    for part in range(2):
        count = ny if part == 0 else nx
        for o in range(1, count):
            second(part, o).wait_recv()
        for d in range(half_z):
            acc = keep_2[part * half_z + d]
            for o in range(1, count):
                acc += recv_2[part, o - 1, d].astype(F32)
            keep_2[part * half_z + d] = acc
            send_3[part * half_z + d] = acc.astype(BF16)

    def start_third(o, _):
        third(o).start()
        return 0

    lax.fori_loop(1, nz, start_third, 0)
    acc = keep_2[z]
    for o in range(1, nz):
        third(o).wait_recv()
        acc += recv_3[o - 1].astype(F32)
    rows = groups * 8
    wide = jnp.concatenate([acc[0:rows], acc[rows : 2 * rows]], axis=1)
    features = wide.astype(BF16)
    feat_ref[...] = features

    rounded = features.astype(F32)
    column = jnp.sum(rounded * rounded, axis=1, keepdims=True)
    diagonal = lax.broadcasted_iota(jnp.int32, (rows, 256), 0) == lax.broadcasted_iota(
        jnp.int32, (rows, 256), 1
    )
    feat_row = jnp.sum(jnp.where(diagonal, column, 0.0), axis=0, keepdims=True)
    padded = jnp.concatenate([rounded, jnp.zeros((8, 256), F32)], axis=0).astype(BF16)
    sub = lax.broadcasted_iota(jnp.int32, (8, 256), 0)

    def dots_copy(o):
        to = plane(lax.div(o, nx), lax.rem(o, nx))
        return remote(
            send_d.at[to], recv_d.at[o], ds_sem.at[o], dr_sem.at[o], to, par
        )

    def dots(o, _):
        b = plane(lax.div(o, nx), lax.rem(o, nx))
        part = lax.dot_general(
            padded, val_v[b], (((1,), (1,)), ((), ())), preferred_element_type=F32
        )
        send_d[b, 0:rows] = part[0:rows]
        send_d[b, rows : rows + 8] = jnp.where(
            sub == 0, val_sq[b], jnp.where(sub == 1, feat_row, 0.0)
        )

        @pl.when(o != 0)
        def _():
            dots_copy(o).start()

        return 0

    lax.fori_loop(0, ex_n, dots, 0)

    def add_dots(o, total):
        dots_copy(o).wait_recv()
        return total + recv_d[o]

    total = lax.fori_loop(1, ex_n, add_dots, send_d[ex])
    feat_sq = jnp.sum(
        jnp.where(diagonal, total[rows + 1 : rows + 2], 0.0), axis=1, keepdims=True
    )
    factor = float(256 * ex_n) ** 0.5
    score_ref[...] = (
        factor * total[0:rows]
        * lax.rsqrt(feat_sq + 1e-06)
        * lax.rsqrt(total[rows : rows + 1] + 1e-06)
    )

    def sent_plane(o, _):
        for g in range(groups):
            a2a(g, o).wait_send()
        dots_copy(o).wait_send()
        return 0

    lax.fori_loop(1, ex_n, sent_plane, 0)

    def sent_core(t, _):
        core_copy(t).wait_send()
        return 0

    lax.fori_loop(0, ex_n, sent_core, 0)
    for k in range(ring_plus + 1):
        val_cross(k, 1).wait_send()
        if k >= 1:
            val_hop(k, 1).wait_send()
        if 1 <= k <= ring_minus:
            val_cross(k, -1).wait_send()
            val_hop(k, -1).wait_send()
    for dx in range(1, nx):
        for dy in range(ny):
            first_x(dy, dx).wait_send()
    for dy in range(1, ny):
        for dx in range(nx):
            first_y(dy, dx).wait_send()
    for o in range(1, ny):
        second(0, o).wait_send()
    for o in range(1, nx):
        second(1, o).wait_send()
    for o in range(1, nz):
        third(o).wait_send()


def shards(ny, nx, nz, adapter_inputs, output_gradient, lengths, projection, validation):
    count, tokens, rank = adapter_inputs.shape
    width = output_gradient.shape[2]
    ex_n, par_n = ny * nx, nz * 2
    groups = count // 8
    vm, dma = pltpu.VMEM, pltpu.SemaphoreType.DMA
    far = max(ny, nx)
    scratch = [
        vm((count, tokens, rank), BF16),
        vm((count, tokens, width), BF16),
        vm(projection.shape, BF16),
        vm((par_n, 256, 256), BF16),
        vm((8 * ex_n * 8, 128), F32),
        vm((groups, ex_n, 16, 512), BF16),
        vm((groups, ex_n, 16, 512), BF16),
        vm((groups * ex_n * 8, 1024), BF16),
        vm((LAG + 1, nz, 2, 2 * groups, 8, 128), F32),
        vm((ex_n, nz, 48, 128), BF16),
        vm((ex_n, nz, 48, 128), BF16),
        vm((2, far - 1, far, nz // 2, 48, 128), BF16),
        vm((2, far - 1, far, nz // 2, 48, 128), BF16),
        vm((2, far, nz // 2, 48, 128), F32),
        vm((2, far - 1, nz // 2, 48, 128), BF16),
        vm((2, far - 1, nz // 2, 48, 128), BF16),
        vm((nz, 48, 128), F32),
        vm((nz, 48, 128), BF16),
        vm((nz - 1, 48, 128), BF16),
        vm((par_n, 8, 256), F32),
        vm((ex_n, 32, 256), F32),
        vm((ex_n, 32, 256), F32),
        dma((groups,)),
        dma((groups,)),
        dma((8, 2)),
        dma(()),
        dma((groups, ex_n)),
        dma((groups, ex_n)),
        dma((nz + 1,)),
        dma((nz + 1,)),
        dma((nz + 1,)),
        dma((nz + 1,)),
        dma((ex_n,)),
        dma((ex_n,)),
        dma((2, far - 1, far)),
        dma((2, far - 1, far)),
        dma((2, far - 1)),
        dma((2, far - 1)),
        dma((nz - 1,)),
        dma((nz - 1,)),
        dma((ex_n,)),
        dma((ex_n,)),
    ]
    anywhere = pl.BlockSpec(memory_space=pl.ANY)
    local = pl.BlockSpec(memory_space=pltpu.VMEM)
    return pl.pallas_call(
        functools.partial(kernel, ny, nx, nz, groups, rank),
        out_shape=(
            jax.ShapeDtypeStruct((count, 256), BF16),
            jax.ShapeDtypeStruct((count, 256), F32),
        ),
        in_specs=[anywhere, anywhere, pl.BlockSpec(memory_space=pltpu.SMEM), anywhere, anywhere],
        out_specs=(local, local),
        scratch_shapes=scratch,
        compiler_params=pltpu.CompilerParams(
            collective_id=0, has_side_effects=True, vmem_limit_bytes=56 * 1024 * 1024
        ),
        cost_estimate=pl.CostEstimate(
            flops=4_000_000_000, bytes_accessed=13_000_000, transcendentals=0
        ),
    )(adapter_inputs, output_gradient, lengths, projection, validation)


def solution(mesh):
    ex_n, par_n = mesh.shape["ex"], mesh.shape["par"]
    nx = 1
    while nx * nx < ex_n:
        nx *= 2
    in_specs = (
        P("ex", None, None),
        P("ex", None, "par"),
        P("ex"),
        P(("par", "ex"), None),
        P("par", "ex"),
    )
    out_specs = (P("par", "ex"), P("par", "ex"))
    return jax.shard_map(
        functools.partial(shards, ex_n // nx, nx, par_n // 2),
        mesh=mesh,
        in_specs=in_specs,
        out_specs=out_specs,
        check_vma=False,
    )
```

```python
import functools

import jax
import jax.numpy as jnp
from jax import lax
from jax.experimental import pallas as pl
from jax.experimental.pallas import tpu as pltpu
from jax.sharding import PartitionSpec as P

MESH = pl.DeviceIdType.MESH
F32 = jnp.float32
BF16 = jnp.bfloat16


def kernel(
    ny, nx, nz, groups, rank,
    ai_hbm, og_hbm, len_ref, proj_hbm, val_hbm,
    feat_ref, score_ref,
    ai_v, og_v, proj_v, val_v, stage_v, send_a, recv_a, lhs, prod, recv_c,
    send_x, recv_x, keep_x, send_y, recv_y, keep_y, send_2, recv_2, keep_2,
    send_3, recv_3, val_sq, send_d, recv_d,
    ai_sem, og_sem, proj_sem, val_sem,
    as_sem, ar_sem, vs_sem, vr_sem, ws_sem, wr_sem, cs_sem, cr_sem,
    sx_sem, rx_sem, sy_sem, ry_sem, s2_sem, r2_sem, s3_sem, r3_sem, ds_sem, dr_sem,
):
    ex_n = ny * nx
    ex = lax.axis_index("ex")
    par = lax.axis_index("par")
    y, x = lax.div(ex, nx), lax.rem(ex, nx)
    z, core = lax.div(par, 2), lax.rem(par, 2)
    tokens = ai_v.shape[2]
    half_z = nz // 2

    def plane(oy, ox):
        return lax.rem(y + oy, ny) * nx + lax.rem(x + ox, nx)

    def depth(oz):
        return lax.rem(z + oz + nz, nz)

    def remote(src, dst, ssem, rsem, to_ex, to_par):
        return pltpu.make_async_remote_copy(
            src_ref=src, dst_ref=dst, send_sem=ssem, recv_sem=rsem,
            device_id=(to_ex, to_par), device_id_type=MESH,
        )

    for g in range(groups):
        rows = pl.ds(g * 8, 8)
        pltpu.make_async_copy(ai_hbm.at[rows], ai_v.at[rows], ai_sem.at[g]).start()
        pltpu.make_async_copy(og_hbm.at[rows], og_v.at[rows], og_sem.at[g]).start()
    val_copy = pltpu.make_async_copy(val_hbm, val_v.at[par], val_sem)
    val_copy.start()

    def proj_copy(s, q):
        return pltpu.make_async_copy(
            proj_hbm.at[pl.ds((q * 8 + s) * rank, rank)],
            proj_v.at[pl.ds(s * 2 * rank + q * rank, rank)],
            proj_sem.at[s, q],
        )

    for s in range(8):
        for q in range(2):
            proj_copy(s, q).start()

    barrier = pltpu.get_barrier_semaphore()

    def greet(to_ex, to_par):
        pl.semaphore_signal(barrier, inc=1, device_id=(to_ex, to_par), device_id_type=MESH)

    def greet_plane(o, _):
        greet(plane(lax.div(o, nx), lax.rem(o, nx)), par)
        return 0

    lax.fori_loop(1, ex_n, greet_plane, 0)

    def greet_depth(o, _):
        greet(ex, depth(o) * 2 + core)
        return 0

    lax.fori_loop(1, nz, greet_depth, 0)
    greet(ex, z * 2 + 1 - core)

    ring_plus, ring_minus = nz // 2, (nz - 1) // 2

    def val_hop(k, sign):
        slot = depth(-sign * (k - 1)) * 2 + core
        sem = k if sign > 0 else ring_plus + k
        return remote(
            val_v.at[slot], val_v.at[slot], vs_sem.at[sem], vr_sem.at[sem], ex, depth(sign) * 2 + core
        )

    def val_cross(k, sign):
        slot = depth(-sign * k) * 2 + core
        sem = k if sign > 0 else ring_plus + k
        return remote(
            val_v.at[slot], val_v.at[slot], ws_sem.at[sem], wr_sem.at[sem], ex, z * 2 + 1 - core
        )

    def val_point(k):
        if k == 0:
            val_copy.wait()
            val_cross(0, 1).start()
        else:
            if k <= ring_plus:
                val_hop(k, 1).wait_recv()
                val_cross(k, 1).start()
            if k <= ring_minus:
                val_hop(k, -1).wait_recv()
                val_cross(k, -1).start()
        if k + 1 <= ring_plus:
            val_hop(k + 1, 1).start()
        if k + 1 <= ring_minus:
            val_hop(k + 1, -1).start()

    lane = lax.broadcasted_iota(jnp.int32, (ex_n, 8, 128), 2)

    def a2a(g, o):
        to = plane(lax.div(o, nx), lax.rem(o, nx))
        return remote(
            send_a.at[g, to], recv_a.at[g, ex], as_sem.at[g, o], ar_sem.at[g, o], to, par
        )

    for g in range(groups):
        rows = pl.ds(g * 8, 8)
        pltpu.make_async_copy(ai_hbm.at[rows], ai_v.at[rows], ai_sem.at[g]).wait()
        pltpu.make_async_copy(og_hbm.at[rows], og_v.at[rows], og_sem.at[g]).wait()

        def gradient(e, _, g=g):
            m = g * 8 + e
            live = lax.broadcasted_iota(jnp.int32, (rank, tokens), 1) < len_ref[m]
            acts = jnp.where(live, ai_v[m].astype(F32), 0.0).astype(BF16)
            out = lax.dot_general(
                og_v[m], jnp.concatenate([acts, acts], axis=0),
                (((0,), (1,)), ((), ())), preferred_element_type=F32,
            )
            out = out.reshape(ex_n, 2, 8, 2 * rank)
            both = jnp.where(lane < rank, out[:, 0], out[:, 1])
            stage_v[pl.ds(pl.multiple_of(e * ex_n * 8, ex_n * 8), ex_n * 8), :] = both.reshape(
                ex_n * 8, 2 * rank
            )
            return 0

        lax.fori_loop(0, 8, gradient, 0)

        def pack(j, _, g=g):
            for q in range(4):
                low = stage_v[pl.ds(j * 8 + q, 8, stride=ex_n * 8), :]
                high = stage_v[pl.ds(j * 8 + q + 4, 8, stride=ex_n * 8), :]
                send_a[g, j, :, q * 128 : (q + 1) * 128] = jnp.concatenate(
                    [low, high], axis=0
                ).astype(BF16)
            return 0

        lax.fori_loop(0, ex_n, pack, 0)
        recv_a[g, ex] = send_a[g, ex]
        if g == 0:
            pl.semaphore_wait(barrier, ex_n - 1 + nz - 1 + 1)

        def send(o, _, g=g):
            a2a(g, o).start()
            return 0

        lax.fori_loop(1, ex_n, send, 0)
        if g == 0:
            val_point(0)

    def row_of(u):
        return lax.rem(lax.rem(u, ny) + 1, ny)

    def core_copy(u):
        return remote(
            prod.at[u, 1 - core], recv_c.at[u], cs_sem.at[u], cr_sem.at[u], ex, z * 2 + 1 - core
        )

    def first_x(g, dy, dx):
        return remote(
            send_x.at[g, dy, dx - 1], recv_x.at[g, dy, dx - 1],
            sx_sem.at[g, dy, dx - 1], rx_sem.at[g, dy, dx - 1], plane(0, dx), par,
        )

    def first_y(g, dy):
        return remote(
            send_y.at[g, dy - 1], recv_y.at[g, dy - 1],
            sy_sem.at[g, dy - 1], ry_sem.at[g, dy - 1], plane(dy, 0), par,
        )

    def pass_on(u):
        g, dy = lax.div(u, ny), row_of(u)
        core_copy(u).wait_recv()
        for dx in [*range(1, nx), 0]:
            xx = lax.rem(x + dx, nx)
            total = prod[u, core, xx, 0:half_z] + recv_c[u, xx, 0:half_z]
            if dx == 0:
                keep_x[g, dy] = total
            else:
                send_x[g, dy, dx - 1] = total.astype(BF16)
                first_x(g, dy, dx).start()

        @pl.when(dy == 0)
        def _():
            for xx in range(nx):
                keep_y[g, xx] = prod[u, core, xx, half_z:nz] + recv_c[u, xx, half_z:nz]

        @pl.when(dy != 0)
        def _():
            for xx in range(nx):
                send_y[g, dy - 1, xx] = (
                    prod[u, core, xx, half_z:nz] + recv_c[u, xx, half_z:nz]
                ).astype(BF16)
            first_y(g, dy).start()

    def chunk(u, _):
        g = lax.div(u, ny)
        yy = lax.rem(y + row_of(u), ny)
        left = lhs[pl.ds(pl.multiple_of(g * ex_n * 8, 16), ex_n * 8), :]
        for xx in range(nx):
            out = jnp.dot(
                left, proj_v[:, pl.ds(pl.multiple_of((yy * nx + xx) * 256, 256), 256)],
                preferred_element_type=F32,
            )
            for l in range(2):
                part = out[:, l * 128 : (l + 1) * 128].reshape(nz, 2, 8, 128)
                for c in range(2):
                    prod[u, c, xx, :, l * 8 : (l + 1) * 8, :] = part[:, c]
        core_copy(u).start()

        @pl.when(u > 0)
        def _():
            pass_on(u - 1)

        return 0

    def second(part, g, o):
        to = plane(o, 0) if part == 0 else plane(0, o)
        return remote(
            send_2.at[part, g, o - 1], recv_2.at[part, g, o - 1],
            s2_sem.at[part, g, o - 1], r2_sem.at[part, g, o - 1], to, par,
        )

    def pass_second(g):
        for dy in range(1, ny):
            first_y(g, dy).wait_recv()
        for o in [*range(1, nx), 0]:
            for dx in range(1, nx):
                first_x(g, o, dx).wait_recv()
            acc = keep_x[g, o]
            for dx in range(1, nx):
                acc += recv_x[g, o, dx - 1].astype(F32)
            if o == 0:
                keep_2[0:half_z, g] = acc
            else:
                send_2[0, g, o - 1] = acc.astype(BF16)
                second(0, g, o).start()
            xx = lax.rem(x + o, nx)
            acc = keep_y[g, xx]
            for dy in range(1, ny):
                acc += recv_y[g, dy - 1, xx].astype(F32)
            if o == 0:
                keep_2[half_z:nz, g] = acc
            else:
                send_2[1, g, o - 1] = acc.astype(BF16)
                second(1, g, o).start()

    def end_second(g):
        for part in range(2):
            own = slice(0, half_z) if part == 0 else slice(half_z, nz)
            acc = keep_2[own, g]
            for o in range(1, nx):
                second(part, g, o).wait_recv()
                acc += recv_2[part, g, o - 1].astype(F32)
            keep_2[own, g] = acc
            send_3[own, g] = acc.astype(BF16)

    ones = jnp.ones((16, 256), BF16)

    def val_norm(b, _):
        wide = val_v[b].astype(F32)
        sq = wide * wide
        high = sq.astype(BF16)
        low = (sq - high.astype(F32)).astype(BF16)
        dims = (((1,), (1,)), ((), ()))
        val_sq[b] = (
            lax.dot_general(ones, high, dims, preferred_element_type=F32)
            + lax.dot_general(ones, low, dims, preferred_element_type=F32)
        )[0:8]
        return 0

    for g in range(groups):
        def arrive(o, _, g=g):
            a2a(g, o).wait_recv()
            return 0

        lax.fori_loop(1, ex_n, arrive, 0)

        def gather(t, _, g=g):
            pair = recv_a[g, pl.ds(2 * t, 2)].astype(F32)
            place = pl.ds(pl.multiple_of(g * ex_n * 8 + t * 16, 16), 16)
            for h in range(2):
                lhs[place, h * 512 : (h + 1) * 512] = jnp.concatenate(
                    [pair[0, h * 8 : h * 8 + 8], pair[1, h * 8 : h * 8 + 8]], axis=0
                ).astype(BF16)
            return 0

        lax.fori_loop(0, ex_n // 2, gather, 0)
        if g == 0:
            for s in range(8):
                for q in range(2):
                    proj_copy(s, q).wait()
        if g + 1 <= ring_plus:
            val_point(g + 1)
        lax.fori_loop(g * ny, (g + 1) * ny, chunk, 0)
        if g >= 1:
            pass_second(g - 1)
    pass_on(groups * ny - 1)
    for k in range(groups + 1, ring_plus + 1):
        val_point(k)
    for k in range(ring_plus + 1):
        val_cross(k, 1).wait_recv()
        if 1 <= k <= ring_minus:
            val_cross(k, -1).wait_recv()
    lax.fori_loop(0, val_v.shape[0], val_norm, 0)
    pass_second(groups - 1)
    for g in range(groups):
        end_second(g)

    def third(o):
        return remote(
            send_3.at[depth(o)], recv_3.at[o - 1], s3_sem.at[o - 1], r3_sem.at[o - 1],
            ex, depth(o) * 2 + core,
        )

    def start_third(o, _):
        third(o).start()
        return 0

    lax.fori_loop(1, nz, start_third, 0)
    acc = keep_2[z]
    for o in range(1, nz):
        third(o).wait_recv()
        acc += recv_3[o - 1].astype(F32)
    rows = groups * 8
    wide = jnp.concatenate(
        [
            jnp.concatenate([acc[g, l * 8 : (l + 1) * 8] for g in range(groups)], axis=0)
            for l in range(2)
        ],
        axis=1,
    )
    features = wide.astype(BF16)
    feat_ref[...] = features

    rounded = features.astype(F32)
    column = jnp.sum(rounded * rounded, axis=1, keepdims=True)
    diagonal = lax.broadcasted_iota(jnp.int32, (rows, 256), 0) == lax.broadcasted_iota(
        jnp.int32, (rows, 256), 1
    )
    feat_row = jnp.sum(jnp.where(diagonal, column, 0.0), axis=0, keepdims=True)
    padded = jnp.concatenate([rounded, jnp.zeros((8, 256), F32)], axis=0).astype(BF16)
    sub = lax.broadcasted_iota(jnp.int32, (8, 256), 0)

    def split(row):
        first = row.astype(BF16).astype(F32)
        second_ = (row - first).astype(BF16).astype(F32)
        return first, second_, row - first - second_

    feat_rows = split(feat_row)

    def dots_copy(o):
        to = plane(lax.div(o, nx), lax.rem(o, nx))
        return remote(
            send_d.at[to], recv_d.at[o], ds_sem.at[o], dr_sem.at[o], to, par
        )

    def dots(o, _):
        b = plane(lax.div(o, nx), lax.rem(o, nx))
        part = lax.dot_general(
            padded, val_v[b], (((1,), (1,)), ((), ())), preferred_element_type=F32
        )
        extra = jnp.zeros((8, 256), F32)
        for k, row in enumerate((*split(val_sq[b]), *feat_rows)):
            extra = jnp.where(sub == k, row, extra)
        send_d[b] = jnp.concatenate([part[0:rows], extra], axis=0).astype(BF16)

        @pl.when(o != 0)
        def _():
            dots_copy(o).start()

        return 0

    lax.fori_loop(0, ex_n, dots, 0)

    def add_dots(o, total):
        dots_copy(o).wait_recv()
        return total + recv_d[o].astype(F32)

    total = lax.fori_loop(1, ex_n, add_dots, send_d[ex].astype(F32))
    val_row = total[rows : rows + 1] + total[rows + 1 : rows + 2] + total[rows + 2 : rows + 3]
    feat_row = total[rows + 3 : rows + 4] + total[rows + 4 : rows + 5] + total[rows + 5 : rows + 6]
    feat_sq = jnp.sum(jnp.where(diagonal, feat_row, 0.0), axis=1, keepdims=True)
    factor = float(256 * ex_n) ** 0.5
    score_ref[...] = (
        factor * total[0:rows] * lax.rsqrt(feat_sq + 1e-06) * lax.rsqrt(val_row + 1e-06)
    )

    def sent_plane(o, _):
        for g in range(groups):
            a2a(g, o).wait_send()
        dots_copy(o).wait_send()
        return 0

    lax.fori_loop(1, ex_n, sent_plane, 0)

    def sent_core(u, _):
        core_copy(u).wait_send()
        return 0

    lax.fori_loop(0, groups * ny, sent_core, 0)
    for k in range(ring_plus + 1):
        val_cross(k, 1).wait_send()
        if k >= 1:
            val_hop(k, 1).wait_send()
        if 1 <= k <= ring_minus:
            val_cross(k, -1).wait_send()
            val_hop(k, -1).wait_send()
    for g in range(groups):
        for dx in range(1, nx):
            for dy in range(ny):
                first_x(g, dy, dx).wait_send()
        for dy in range(1, ny):
            first_y(g, dy).wait_send()
        for o in range(1, nx):
            second(0, g, o).wait_send()
            second(1, g, o).wait_send()
    for o in range(1, nz):
        third(o).wait_send()


def shards(ny, nx, nz, adapter_inputs, output_gradient, lengths, projection, validation):
    adapter_inputs = jnp.swapaxes(adapter_inputs, 1, 2)
    count, rank, tokens = adapter_inputs.shape
    width = output_gradient.shape[2]
    ex_n, par_n = ny * nx, nz * 2
    groups = count // 8
    vm, dma = pltpu.VMEM, pltpu.SemaphoreType.DMA
    half_z = nz // 2
    x_block, y_block = (half_z, 16, 128), (nx, half_z, 16, 128)
    scratch = [
        vm((count, rank, tokens), BF16),
        vm((count, tokens, width), BF16),
        vm(projection.shape, BF16),
        vm((par_n, 256, 256), BF16),
        vm((8 * ex_n * 8, 128), F32),
        vm((groups, ex_n, 16, 512), BF16),
        vm((groups, ex_n, 16, 512), BF16),
        vm((groups * ex_n * 8, 1024), BF16),
        vm((groups * ny, 2, nx, nz, 16, 128), F32),
        vm((groups * ny, nx, nz, 16, 128), F32),
        vm((groups, ny, nx - 1, *x_block), BF16),
        vm((groups, ny, nx - 1, *x_block), BF16),
        vm((groups, ny, *x_block), F32),
        vm((groups, ny - 1, *y_block), BF16),
        vm((groups, ny - 1, *y_block), BF16),
        vm((groups, *y_block), F32),
        vm((2, groups, nx - 1, *x_block), BF16),
        vm((2, groups, nx - 1, *x_block), BF16),
        vm((nz, groups, 16, 128), F32),
        vm((nz, groups, 16, 128), BF16),
        vm((nz - 1, groups, 16, 128), BF16),
        vm((par_n, 8, 256), F32),
        vm((ex_n, 32, 256), BF16),
        vm((ex_n, 32, 256), BF16),
        dma((groups,)),
        dma((groups,)),
        dma((8, 2)),
        dma(()),
        dma((groups, ex_n)),
        dma((groups, ex_n)),
        dma((nz + 1,)),
        dma((nz + 1,)),
        dma((nz + 1,)),
        dma((nz + 1,)),
        dma((groups * ny,)),
        dma((groups * ny,)),
        dma((groups, ny, nx - 1)),
        dma((groups, ny, nx - 1)),
        dma((groups, ny - 1)),
        dma((groups, ny - 1)),
        dma((2, groups, nx - 1)),
        dma((2, groups, nx - 1)),
        dma((nz - 1,)),
        dma((nz - 1,)),
        dma((ex_n,)),
        dma((ex_n,)),
    ]
    anywhere = pl.BlockSpec(memory_space=pl.ANY)
    local = pl.BlockSpec(memory_space=pltpu.VMEM)
    return pl.pallas_call(
        functools.partial(kernel, ny, nx, nz, groups, rank),
        out_shape=(
            jax.ShapeDtypeStruct((count, 256), BF16),
            jax.ShapeDtypeStruct((count, 256), F32),
        ),
        in_specs=[anywhere, anywhere, pl.BlockSpec(memory_space=pltpu.SMEM), anywhere, anywhere],
        out_specs=(local, local),
        scratch_shapes=scratch,
        compiler_params=pltpu.CompilerParams(
            collective_id=0, has_side_effects=True, vmem_limit_bytes=56 * 1024 * 1024
        ),
        cost_estimate=pl.CostEstimate(
            flops=4_000_000_000, bytes_accessed=13_000_000, transcendentals=0
        ),
    )(adapter_inputs, output_gradient, lengths, projection, validation)


def solution(mesh):
    ex_n, par_n = mesh.shape["ex"], mesh.shape["par"]
    nx = 1
    while nx * nx < ex_n:
        nx *= 2
    in_specs = (
        P("ex", None, None),
        P("ex", None, "par"),
        P("ex"),
        P(("par", "ex"), None),
        P("par", "ex"),
    )
    out_specs = (P("par", "ex"), P("par", "ex"))
    return jax.shard_map(
        functools.partial(shards, ex_n // nx, nx, par_n // 2),
        mesh=mesh,
        in_specs=in_specs,
        out_specs=out_specs,
        check_vma=False,
    )
```

```python
import functools

import jax
import jax.numpy as jnp
from jax import lax
from jax.experimental import pallas as pl
from jax.experimental.pallas import tpu as pltpu
from jax.sharding import PartitionSpec as P

MESH = pl.DeviceIdType.MESH
F32 = jnp.float32
BF16 = jnp.bfloat16


def kernel(
    ny, nx, nz, groups, rank,
    ai_hbm, og_hbm, len_hbm, proj_hbm, val_hbm,
    out_ref,
    len_ref, ai_v, og_v, proj_v, val_v, stage_v, send_a, recv_a, lhs, prod, recv_c,
    send_x, recv_x, keep_x, send_y, recv_y, keep_y, send_2, recv_2, keep_2,
    send_3, recv_3, val_sq, send_d, recv_d,
    len_sem, ai_sem, og_sem, proj_sem, val_sem,
    as_sem, ar_sem, vs_sem, vr_sem, ws_sem, wr_sem, cs_sem, cr_sem,
    sx_sem, rx_sem, sy_sem, ry_sem, s2_sem, r2_sem, s3_sem, r3_sem, ds_sem, dr_sem,
):
    ex_n = ny * nx
    ex = lax.axis_index("ex")
    par = lax.axis_index("par")
    y, x = lax.div(ex, nx), lax.rem(ex, nx)
    z, core = lax.div(par, 2), lax.rem(par, 2)
    tokens = ai_v.shape[2]
    half_z = nz // 2

    def plane(oy, ox):
        return lax.rem(y + oy, ny) * nx + lax.rem(x + ox, nx)

    def depth(oz):
        return lax.rem(z + oz + nz, nz)

    def remote(src, dst, ssem, rsem, to_ex, to_par):
        return pltpu.make_async_remote_copy(
            src_ref=src, dst_ref=dst, send_sem=ssem, recv_sem=rsem,
            device_id=(to_ex, to_par), device_id_type=MESH,
        )

    def load(g):
        rows = pl.ds(g * 8, 8)
        pltpu.make_async_copy(og_hbm.at[rows], og_v.at[rows], og_sem.at[g]).start()
        pltpu.make_async_copy(ai_hbm.at[rows], ai_v.at[rows], ai_sem.at[g]).start()

    load(0)
    len_copy = pltpu.make_async_copy(len_hbm, len_ref, len_sem)
    len_copy.start()

    barrier = pltpu.get_barrier_semaphore()

    def greet(to_ex, to_par):
        pl.semaphore_signal(barrier, inc=1, device_id=(to_ex, to_par), device_id_type=MESH)

    def greet_plane(o, _):
        greet(plane(lax.div(o, nx), lax.rem(o, nx)), par)
        return 0

    lax.fori_loop(1, ex_n, greet_plane, 0)

    def greet_depth(o, _):
        greet(ex, depth(o) * 2 + core)
        return 0

    lax.fori_loop(1, nz, greet_depth, 0)
    greet(ex, z * 2 + 1 - core)

    def whole(src, dst, ssem, rsem):
        return remote(src, dst, ssem, rsem, ex, z * 2 + 1 - core)

    for g in range(1, groups):
        load(g)
    val_copy = pltpu.make_async_copy(val_hbm, val_v.at[par], val_sem)
    val_copy.start()

    def proj_copy(s, q):
        return pltpu.make_async_copy(
            proj_hbm.at[pl.ds((q * 8 + s) * rank, rank)],
            proj_v.at[pl.ds(s * 2 * rank + q * rank, rank)],
            proj_sem,
        )

    ring_plus, ring_minus = nz // 2, (nz - 1) // 2

    def val_hop(k, sign):
        slot = depth(-sign * (k - 1)) * 2 + core
        sem = k if sign > 0 else ring_plus + k
        return remote(
            val_v.at[slot], val_v.at[slot], vs_sem, vr_sem.at[sem], ex, depth(sign) * 2 + core
        )

    def val_cross(k, sign):
        slot = depth(-sign * k) * 2 + core
        sem = k if sign > 0 else ring_plus + k
        return remote(
            val_v.at[slot], val_v.at[slot], ws_sem, wr_sem.at[sem], ex, z * 2 + 1 - core
        )

    def val_point(k):
        if k == 0:
            val_copy.wait()
            val_cross(0, 1).start()
        else:
            if k <= ring_plus:
                val_hop(k, 1).wait_recv()
                val_cross(k, 1).start()
            if k <= ring_minus:
                val_hop(k, -1).wait_recv()
                val_cross(k, -1).start()
        if k + 1 <= ring_plus:
            val_hop(k + 1, 1).start()
        if k + 1 <= ring_minus:
            val_hop(k + 1, -1).start()

    lane = lax.broadcasted_iota(jnp.int32, (ex_n, 8, 128), 2)

    def a2a(g, o):
        to = plane(lax.div(o, nx), lax.rem(o, nx))
        return remote(
            send_a.at[g, to], recv_a.at[g, ex], as_sem.at[g], ar_sem.at[g], to, par
        )

    for g in range(groups):
        rows = pl.ds(g * 8, 8)
        pltpu.make_async_copy(ai_hbm.at[rows], ai_v.at[rows], ai_sem.at[g]).wait()
        pltpu.make_async_copy(og_hbm.at[rows], og_v.at[rows], og_sem.at[g]).wait()

        def gradient(e, _, g=g):
            m = g * 8 + e
            live = lax.broadcasted_iota(jnp.int32, (rank, tokens), 1) < len_ref[m]
            acts = jnp.where(live, ai_v[m].astype(F32), 0.0).astype(BF16)
            out = lax.dot_general(
                og_v[m], jnp.concatenate([acts, acts], axis=0),
                (((0,), (1,)), ((), ())), preferred_element_type=F32,
            )
            out = out.reshape(ex_n, 2, 8, 2 * rank)
            both = jnp.where(lane < rank, out[:, 0], out[:, 1])
            stage_v[pl.ds(pl.multiple_of(e * ex_n * 8, ex_n * 8), ex_n * 8), :] = both.reshape(
                ex_n * 8, 2 * rank
            )
            return 0

        if g == 0:
            len_copy.wait()
        lax.fori_loop(0, 8, gradient, 0, unroll=4)

        def pack(j, _, g=g):
            for q in range(4):
                low = stage_v[pl.ds(j * 8 + q, 8, stride=ex_n * 8), :]
                high = stage_v[pl.ds(j * 8 + q + 4, 8, stride=ex_n * 8), :]
                send_a[g, j, :, q * 128 : (q + 1) * 128] = jnp.concatenate(
                    [low, high], axis=0
                ).astype(BF16)
            return 0

        lax.fori_loop(0, ex_n, pack, 0, unroll=4)
        recv_a[g, ex] = send_a[g, ex]
        if g == 0:
            pl.semaphore_wait(barrier, ex_n - 1 + nz - 1 + 1)

        def send(o, _, g=g):
            a2a(g, o).start()
            return 0

        lax.fori_loop(1, ex_n, send, 0)
        if g == 0:
            for s in range(8):
                for q in range(2):
                    proj_copy(s, q).start()
            val_point(0)
        if g == groups - 1:
            val_point(1)

    def row_of(u):
        return lax.rem(lax.rem(u, ny) + 1, ny)

    def core_copy(u):
        return remote(
            prod.at[u, 1 - core], recv_c.at[u], cs_sem, cr_sem.at[u], ex, z * 2 + 1 - core
        )

    def first_x(g, dy, dx):
        return remote(
            send_x.at[g, dy, dx - 1], recv_x.at[g, dy, dx - 1],
            sx_sem, rx_sem.at[g, dy], plane(0, dx), par,
        )

    def first_y(g, dy):
        return remote(
            send_y.at[g, dy - 1], recv_y.at[g, dy - 1],
            sy_sem, ry_sem.at[g], plane(dy, 0), par,
        )

    def pass_on(u):
        g, dy = lax.div(u, ny), row_of(u)
        core_copy(u).wait_recv()
        for dx in [*range(1, nx), 0]:
            xx = lax.rem(x + dx, nx)
            total = prod[u, core, xx, 0:half_z] + recv_c[u, xx, 0:half_z]
            if dx == 0:
                keep_x[g, dy] = total
            else:
                send_x[g, dy, dx - 1] = total.astype(BF16)
                first_x(g, dy, dx).start()

        @pl.when(dy == 0)
        def _():
            for xx in range(nx):
                keep_y[g, xx] = prod[u, core, xx, half_z:nz] + recv_c[u, xx, half_z:nz]

        @pl.when(dy != 0)
        def _():
            for xx in range(nx):
                send_y[g, dy - 1, xx] = (
                    prod[u, core, xx, half_z:nz] + recv_c[u, xx, half_z:nz]
                ).astype(BF16)
            first_y(g, dy).start()

    def chunk(u, _):
        g = lax.div(u, ny)
        yy = lax.rem(y + row_of(u), ny)
        left = lhs[pl.ds(pl.multiple_of(g * ex_n * 8, 16), ex_n * 8), :]
        for xx in range(nx):
            out = jnp.dot(
                left, proj_v[:, pl.ds(pl.multiple_of((yy * nx + xx) * 256, 256), 256)],
                preferred_element_type=F32,
            )
            for l in range(2):
                part = out[:, l * 128 : (l + 1) * 128].reshape(nz, 2, 8, 128)
                for c in range(2):
                    prod[u, c, xx, :, l * 8 : (l + 1) * 8, :] = part[:, c]
        core_copy(u).start()
        return 0

    def pass_group(u, _):
        pass_on(u)
        return 0

    def second(part, g, o):
        to = plane(o, 0) if part == 0 else plane(0, o)
        return remote(
            send_2.at[part, g, o - 1], recv_2.at[part, g, o - 1],
            s2_sem, r2_sem.at[part, g], to, par,
        )

    def pass_second(g):
        whole(send_y.at[g], recv_y.at[g], sy_sem, ry_sem.at[g]).wait_recv()
        for o in [*range(1, nx), 0]:
            whole(send_x.at[g, o], recv_x.at[g, o], sx_sem, rx_sem.at[g, o]).wait_recv()
            acc = keep_x[g, o]
            for dx in range(1, nx):
                acc += recv_x[g, o, dx - 1].astype(F32)
            if o == 0:
                keep_2[0:half_z, g] = acc
            else:
                send_2[0, g, o - 1] = acc.astype(BF16)
                second(0, g, o).start()
            xx = lax.rem(x + o, nx)
            acc = keep_y[g, xx]
            for dy in range(1, ny):
                acc += recv_y[g, dy - 1, xx].astype(F32)
            if o == 0:
                keep_2[half_z:nz, g] = acc
            else:
                send_2[1, g, o - 1] = acc.astype(BF16)
                second(1, g, o).start()

    def end_second(g):
        for part in range(2):
            own = slice(0, half_z) if part == 0 else slice(half_z, nz)
            acc = keep_2[own, g]
            whole(
                send_2.at[part, g], recv_2.at[part, g], s2_sem, r2_sem.at[part, g]
            ).wait_recv()
            for o in range(1, nx):
                acc += recv_2[part, g, o - 1].astype(F32)
            keep_2[own, g] = acc
            send_3[own, g] = acc.astype(BF16)

    ones = jnp.ones((16, 256), BF16)

    def val_norm(b):
        wide = val_v[b].astype(F32)
        sq = wide * wide
        high = sq.astype(BF16)
        low = (sq - high.astype(F32)).astype(BF16)
        dims = (((1,), (1,)), ((), ()))
        val_sq[b] = (
            lax.dot_general(ones, high, dims, preferred_element_type=F32)
            + lax.dot_general(ones, low, dims, preferred_element_type=F32)
        )[0:8]

    def norms(k):
        val_cross(k, 1).wait_recv()
        if 1 <= k <= ring_minus:
            val_cross(k, -1).wait_recv()
        for c in range(2):
            val_norm(depth(-k) * 2 + c)
            if 1 <= k <= ring_minus:
                val_norm(depth(k) * 2 + c)

    for g in range(groups):
        blocks = pl.ds(0, ex_n - 1)
        whole(send_a.at[g, blocks], recv_a.at[g, blocks], as_sem.at[g], ar_sem.at[g]).wait_recv()

        def gather(t, _, g=g):
            pair = recv_a[g, pl.ds(2 * t, 2)].astype(F32)
            place = pl.ds(pl.multiple_of(g * ex_n * 8 + t * 16, 16), 16)
            for h in range(2):
                lhs[place, h * 512 : (h + 1) * 512] = jnp.concatenate(
                    [pair[0, h * 8 : h * 8 + 8], pair[1, h * 8 : h * 8 + 8]], axis=0
                ).astype(BF16)
            return 0

        lax.fori_loop(0, ex_n // 2, gather, 0)
        if g == 0:
            pltpu.make_async_copy(proj_hbm, proj_v, proj_sem).wait()
        first = g * ny
        ahead = min(2, ny)
        lax.fori_loop(first, first + ahead, chunk, 0)

        def both(u, _, ahead=ahead):
            chunk(u, 0)
            pass_on(u - ahead)
            return 0

        lax.fori_loop(first + ahead, first + ny, both, 0)
        if g >= 1:
            pass_second(g - 1)
        lax.fori_loop(first + ny - ahead, first + ny, pass_group, 0)
        if 2 <= g + 2 <= ring_plus:
            val_point(g + 2)
            norms(g)
    done = min(groups, max(ring_plus - 1, 0))
    pass_second(groups - 1)
    for g in range(groups - 1):
        end_second(g)
    for k in range(max(groups + 2, 2), ring_plus + 1):
        val_point(k)
    for k in range(done, ring_plus + 1):
        norms(k)
    end_second(groups - 1)

    def third(o):
        return remote(
            send_3.at[depth(o)], recv_3.at[o - 1], s3_sem, r3_sem,
            ex, depth(o) * 2 + core,
        )

    def start_third(o, _):
        third(o).start()
        return 0

    lax.fori_loop(1, nz, start_third, 0)

    for g in range(groups):
        whole(send_a.at[g, blocks], recv_a.at[g, blocks], as_sem.at[g], ar_sem.at[g]).wait_send()
    whole(prod.at[:, 0], recv_c, cs_sem, cr_sem.at[0]).wait_send()
    hops, crosses = val_v.at[pl.ds(0, nz - 1)], val_v.at[pl.ds(0, nz)]
    whole(hops, hops, vs_sem, vr_sem.at[0]).wait_send()
    whole(crosses, crosses, ws_sem, wr_sem.at[0]).wait_send()
    whole(send_x, recv_x, sx_sem, rx_sem.at[0, 0]).wait_send()
    whole(send_y, recv_y, sy_sem, ry_sem.at[0]).wait_send()
    whole(send_2, recv_2, s2_sem, r2_sem.at[0, 0]).wait_send()

    last = whole(send_3.at[pl.ds(0, nz - 1)], recv_3, s3_sem, r3_sem)
    last.wait_recv()
    acc = keep_2[z]
    for o in range(1, nz):
        acc += recv_3[o - 1].astype(F32)
    rows = groups * 8
    wide = jnp.concatenate(
        [
            jnp.concatenate([acc[g, l * 8 : (l + 1) * 8] for g in range(groups)], axis=0)
            for l in range(2)
        ],
        axis=1,
    )
    features = wide.astype(BF16)
    out_ref[0] = features.astype(F32)

    rounded = features.astype(F32)
    column = jnp.sum(rounded * rounded, axis=1, keepdims=True)
    diagonal = lax.broadcasted_iota(jnp.int32, (rows, 256), 0) == lax.broadcasted_iota(
        jnp.int32, (rows, 256), 1
    )
    feat_row = jnp.sum(jnp.where(diagonal, column, 0.0), axis=0, keepdims=True)
    padded = jnp.concatenate([rounded, jnp.zeros((8, 256), F32)], axis=0).astype(BF16)
    sub = lax.broadcasted_iota(jnp.int32, (8, 256), 0)

    def split(row):
        first = row.astype(BF16).astype(F32)
        second_ = (row - first).astype(BF16).astype(F32)
        return first, second_, row - first - second_

    feat_rows = split(feat_row)

    def dots_copy(o):
        to = plane(lax.div(o, nx), lax.rem(o, nx))
        return remote(
            send_d.at[to], recv_d.at[o], ds_sem, dr_sem, to, par
        )

    for o in [*range(ex_n - 1, 0, -1), 0]:
        b = plane(o // nx, o % nx)
        part = lax.dot_general(
            padded, val_v[b], (((1,), (1,)), ((), ())), preferred_element_type=F32
        )
        extra = jnp.zeros((8, 256), F32)
        for k, row in enumerate((*split(val_sq[b]), *feat_rows)):
            extra = jnp.where(sub == k, row, extra)
        send_d[b] = jnp.concatenate([part[0:rows], extra], axis=0).astype(BF16)
        if o != 0:
            dots_copy(o).start()

    total = send_d[ex].astype(F32)
    every = whole(
        send_d.at[pl.ds(0, ex_n - 1)], recv_d.at[pl.ds(1, ex_n - 1)], ds_sem, dr_sem
    )
    every.wait_recv()
    for o in range(1, ex_n):
        total = total + recv_d[o].astype(F32)
    val_row = total[rows : rows + 1] + total[rows + 1 : rows + 2] + total[rows + 2 : rows + 3]
    feat_row = total[rows + 3 : rows + 4] + total[rows + 4 : rows + 5] + total[rows + 5 : rows + 6]
    feat_sq = jnp.sum(jnp.where(diagonal, feat_row, 0.0), axis=1, keepdims=True)
    factor = float(256 * ex_n) ** 0.5
    out_ref[1] = (
        factor * total[0:rows] * lax.rsqrt(feat_sq + 1e-06) * lax.rsqrt(val_row + 1e-06)
    )

    every.wait_send()
    last.wait_send()

def shards(ny, nx, nz, adapter_inputs, output_gradient, lengths, projection, validation):
    adapter_inputs = jnp.swapaxes(adapter_inputs, 1, 2)
    count, rank, tokens = adapter_inputs.shape
    width = output_gradient.shape[2]
    ex_n, par_n = ny * nx, nz * 2
    groups = count // 8
    vm, dma = pltpu.VMEM, pltpu.SemaphoreType.DMA
    half_z = nz // 2
    x_block, y_block = (half_z, 16, 128), (nx, half_z, 16, 128)
    scratch = [
        pltpu.SMEM(lengths.shape, jnp.int32),
        vm((count, rank, tokens), BF16),
        vm((count, tokens, width), BF16),
        vm(projection.shape, BF16),
        vm((par_n, 256, 256), BF16),
        vm((8 * ex_n * 8, 128), F32),
        vm((groups, ex_n, 16, 512), BF16),
        vm((groups, ex_n, 16, 512), BF16),
        vm((groups * ex_n * 8, 1024), BF16),
        vm((groups * ny, 2, nx, nz, 16, 128), F32),
        vm((groups * ny, nx, nz, 16, 128), F32),
        vm((groups, ny, nx - 1, *x_block), BF16),
        vm((groups, ny, nx - 1, *x_block), BF16),
        vm((groups, ny, *x_block), F32),
        vm((groups, ny - 1, *y_block), BF16),
        vm((groups, ny - 1, *y_block), BF16),
        vm((groups, *y_block), F32),
        vm((2, groups, nx - 1, *x_block), BF16),
        vm((2, groups, nx - 1, *x_block), BF16),
        vm((nz, groups, 16, 128), F32),
        vm((nz, groups, 16, 128), BF16),
        vm((nz - 1, groups, 16, 128), BF16),
        vm((par_n, 8, 256), F32),
        vm((ex_n, 32, 256), BF16),
        vm((ex_n, 32, 256), BF16),
        dma(()),
        dma((groups,)),
        dma((groups,)),
        dma(()),
        dma(()),
        dma((groups,)),
        dma((groups,)),
        dma(()),
        dma((nz,)),
        dma(()),
        dma((nz,)),
        dma(()),
        dma((groups * ny,)),
        dma(()),
        dma((groups, ny)),
        dma(()),
        dma((groups,)),
        dma(()),
        dma((2, groups)),
        dma(()),
        dma(()),
        dma(()),
        dma(()),
    ]
    anywhere = pl.BlockSpec(memory_space=pl.ANY)
    local = pl.BlockSpec(memory_space=pltpu.VMEM)
    out = pl.pallas_call(
        functools.partial(kernel, ny, nx, nz, groups, rank),
        out_shape=jax.ShapeDtypeStruct((2, count, 256), F32),
        in_specs=[anywhere, anywhere, anywhere, anywhere, anywhere],
        out_specs=local,
        scratch_shapes=scratch,
        compiler_params=pltpu.CompilerParams(
            collective_id=0, has_side_effects=True, vmem_limit_bytes=56 * 1024 * 1024
        ),
        cost_estimate=pl.CostEstimate(
            flops=4_000_000_000, bytes_accessed=13_000_000, transcendentals=0
        ),
    )(adapter_inputs, output_gradient, lengths, projection, validation)
    return out[0].astype(BF16), out[1]


def solution(mesh):
    ex_n, par_n = mesh.shape["ex"], mesh.shape["par"]
    nx = 1
    while nx * nx < ex_n:
        nx *= 2
    in_specs = (
        P("ex", None, None),
        P("ex", None, "par"),
        P("ex"),
        P(("par", "ex"), None),
        P("par", "ex"),
    )
    out_specs = (P("par", "ex"), P("par", "ex"))
    return jax.shard_map(
        functools.partial(shards, ex_n // nx, nx, par_n // 2),
        mesh=mesh,
        in_specs=in_specs,
        out_specs=out_specs,
        check_vma=False,
    )
```

```python
import functools

import jax
import jax.numpy as jnp
from jax import lax
from jax.experimental import pallas as pl
from jax.experimental.pallas import tpu as pltpu
from jax.sharding import PartitionSpec as P

MESH = pl.DeviceIdType.MESH
F32 = jnp.float32
BF16 = jnp.bfloat16


def kernel(
    ny, nx, nz, groups, rank,
    ai_hbm, og_hbm, len_hbm, proj_hbm, val_hbm,
    out_ref,
    len_ref, ai_v, og_v, proj_v, val_v, stage_v, send_a, recv_a, lhs, prod, recv_c,
    send_x, recv_x, keep_x, send_y, recv_y, keep_y, send_2, recv_2, keep_2,
    send_3, recv_3, val_sq, send_d, recv_d,
    len_sem, ai_sem, og_sem, proj_sem, val_sem,
    as_sem, ar_sem, vs_sem, vr_sem, ws_sem, wr_sem, cs_sem, cr_sem,
    sx_sem, rx_sem, sy_sem, ry_sem, s2_sem, r2_sem, s3_sem, r3_sem, ds_sem, dr_sem,
):
    ex_n = ny * nx
    ex = lax.axis_index("ex")
    par = lax.axis_index("par")
    y, x = lax.div(ex, nx), lax.rem(ex, nx)
    z, core = lax.div(par, 2), lax.rem(par, 2)
    tokens = ai_v.shape[2]
    half_z = nz // 2

    def plane(oy, ox):
        return lax.rem(y + oy, ny) * nx + lax.rem(x + ox, nx)

    def depth(oz):
        return lax.rem(z + oz + nz, nz)

    def remote(src, dst, ssem, rsem, to_ex, to_par):
        return pltpu.make_async_remote_copy(
            src_ref=src, dst_ref=dst, send_sem=ssem, recv_sem=rsem,
            device_id=(to_ex, to_par), device_id_type=MESH,
        )

    def load(g):
        rows = pl.ds(g * 8, 8)
        pltpu.make_async_copy(og_hbm.at[rows], og_v.at[rows], og_sem.at[g]).start()
        pltpu.make_async_copy(ai_hbm.at[rows], ai_v.at[rows], ai_sem.at[g]).start()

    load(0)
    len_copy = pltpu.make_async_copy(len_hbm, len_ref, len_sem)
    len_copy.start()

    barrier = pltpu.get_barrier_semaphore()

    def greet(to_ex, to_par):
        pl.semaphore_signal(barrier, inc=1, device_id=(to_ex, to_par), device_id_type=MESH)

    for o in range(1, ex_n):
        greet(plane(o // nx, o % nx), par)

    for o in range(1, nz):
        greet(ex, depth(o) * 2 + core)
    greet(ex, z * 2 + 1 - core)

    def whole(src, dst, ssem, rsem):
        return remote(src, dst, ssem, rsem, ex, z * 2 + 1 - core)

    for g in range(1, groups):
        load(g)
    val_copy = pltpu.make_async_copy(val_hbm, val_v.at[par], val_sem)
    val_copy.start()

    def proj_copy(s, q):
        return pltpu.make_async_copy(
            proj_hbm.at[pl.ds((q * 8 + s) * rank, rank)],
            proj_v.at[pl.ds(s * 2 * rank + q * rank, rank)],
            proj_sem,
        )

    ring_plus, ring_minus = nz // 2, (nz - 1) // 2

    def val_hop(k, sign):
        slot = depth(-sign * (k - 1)) * 2 + core
        sem = k if sign > 0 else ring_plus + k
        return remote(
            val_v.at[slot], val_v.at[slot], vs_sem, vr_sem.at[sem], ex, depth(sign) * 2 + core
        )

    def val_cross(k, sign):
        slot = depth(-sign * k) * 2 + core
        sem = k if sign > 0 else ring_plus + k
        return remote(
            val_v.at[slot], val_v.at[slot], ws_sem, wr_sem.at[sem], ex, z * 2 + 1 - core
        )

    def val_point(k):
        if k == 0:
            val_copy.wait()
            val_cross(0, 1).start()
        else:
            if k <= ring_plus:
                val_hop(k, 1).wait_recv()
                val_cross(k, 1).start()
            if k <= ring_minus:
                val_hop(k, -1).wait_recv()
                val_cross(k, -1).start()
        if k + 1 <= ring_plus:
            val_hop(k + 1, 1).start()
        if k + 1 <= ring_minus:
            val_hop(k + 1, -1).start()

    lane = lax.broadcasted_iota(jnp.int32, (ex_n, 8, 128), 2)

    def a2a(g, o):
        to = plane(o // nx, o % nx)
        return remote(
            send_a.at[g, to], recv_a.at[g, ex], as_sem.at[g], ar_sem.at[g], to, par
        )

    for g in range(groups):
        rows = pl.ds(g * 8, 8)
        pltpu.make_async_copy(ai_hbm.at[rows], ai_v.at[rows], ai_sem.at[g]).wait()
        pltpu.make_async_copy(og_hbm.at[rows], og_v.at[rows], og_sem.at[g]).wait()

        def gradient(e, _, g=g):
            m = g * 8 + e
            live = lax.broadcasted_iota(jnp.int32, (rank, tokens), 1) < len_ref[m]
            acts = jnp.where(live, ai_v[m].astype(F32), 0.0).astype(BF16)
            out = lax.dot_general(
                og_v[m], jnp.concatenate([acts, acts], axis=0),
                (((0,), (1,)), ((), ())), preferred_element_type=F32,
            )
            out = out.reshape(ex_n, 2, 8, 2 * rank)
            both = jnp.where(lane < rank, out[:, 0], out[:, 1])
            stage_v[pl.ds(pl.multiple_of(e * ex_n * 8, ex_n * 8), ex_n * 8), :] = both.reshape(
                ex_n * 8, 2 * rank
            )
            return 0

        if g == 0:
            len_copy.wait()
        lax.fori_loop(0, 8, gradient, 0, unroll=4)

        def pack(j, _, g=g):
            for q in range(4):
                low = stage_v[pl.ds(j * 8 + q, 8, stride=ex_n * 8), :]
                high = stage_v[pl.ds(j * 8 + q + 4, 8, stride=ex_n * 8), :]
                send_a[g, j, :, q * 128 : (q + 1) * 128] = jnp.concatenate(
                    [low, high], axis=0
                ).astype(BF16)
            return 0

        lax.fori_loop(0, ex_n, pack, 0, unroll=4)
        recv_a[g, ex] = send_a[g, ex]
        if g == 0:
            pl.semaphore_wait(barrier, ex_n - 1 + nz - 1 + 1)

        for o in range(1, ex_n):
            a2a(g, o).start()
        if g == 0:
            for s in range(8):
                for q in range(2):
                    proj_copy(s, q).start()
            val_point(0)
        if g == groups - 1:
            val_point(1)

    def row_of(u):
        return lax.rem(lax.rem(u, ny) + 1, ny)

    def core_copy(u):
        return remote(
            prod.at[u, 1 - core], recv_c.at[u], cs_sem, cr_sem.at[u], ex, z * 2 + 1 - core
        )

    def first_x(g, dy, dx):
        return remote(
            send_x.at[g, dy, dx - 1], recv_x.at[g, dy, dx - 1],
            sx_sem, rx_sem.at[g, dy], plane(0, dx), par,
        )

    def first_y(g, dy):
        return remote(
            send_y.at[g, dy - 1], recv_y.at[g, dy - 1],
            sy_sem, ry_sem.at[g], plane(dy, 0), par,
        )

    def pass_on(u):
        g, dy = lax.div(u, ny), row_of(u)
        core_copy(u).wait_recv()
        for dx in [*range(1, nx), 0]:
            xx = lax.rem(x + dx, nx)
            total = prod[u, core, xx, 0:half_z] + recv_c[u, xx, 0:half_z]
            if dx == 0:
                keep_x[g, dy] = total
            else:
                send_x[g, dy, dx - 1] = total.astype(BF16)
                first_x(g, dy, dx).start()

        @pl.when(dy == 0)
        def _():
            for xx in range(nx):
                keep_y[g, xx] = prod[u, core, xx, half_z:nz] + recv_c[u, xx, half_z:nz]

        @pl.when(dy != 0)
        def _():
            for xx in range(nx):
                send_y[g, dy - 1, xx] = (
                    prod[u, core, xx, half_z:nz] + recv_c[u, xx, half_z:nz]
                ).astype(BF16)
            first_y(g, dy).start()

    def chunk(u, _):
        g = lax.div(u, ny)
        yy = lax.rem(y + row_of(u), ny)
        left = lhs[pl.ds(pl.multiple_of(g * ex_n * 8, 16), ex_n * 8), :]
        for xx in range(nx):
            out = jnp.dot(
                left, proj_v[:, pl.ds(pl.multiple_of((yy * nx + xx) * 256, 256), 256)],
                preferred_element_type=F32,
            )
            for l in range(2):
                part = out[:, l * 128 : (l + 1) * 128].reshape(nz, 2, 8, 128)
                for c in range(2):
                    prod[u, c, xx, :, l * 8 : (l + 1) * 8, :] = part[:, c]
        core_copy(u).start()
        return 0

    def pass_group(u, _):
        pass_on(u)
        return 0

    def second(part, g, o):
        to = plane(o, 0) if part == 0 else plane(0, o)
        return remote(
            send_2.at[part, g, o - 1], recv_2.at[part, g, o - 1],
            s2_sem, r2_sem.at[part, g], to, par,
        )

    def pass_second(g):
        whole(send_y.at[g], recv_y.at[g], sy_sem, ry_sem.at[g]).wait_recv()
        for o in [*range(1, nx), 0]:
            whole(send_x.at[g, o], recv_x.at[g, o], sx_sem, rx_sem.at[g, o]).wait_recv()
            acc = keep_x[g, o]
            for dx in range(1, nx):
                acc += recv_x[g, o, dx - 1].astype(F32)
            if o == 0:
                keep_2[0:half_z, g] = acc
            else:
                send_2[0, g, o - 1] = acc.astype(BF16)
                second(0, g, o).start()
            xx = lax.rem(x + o, nx)
            acc = keep_y[g, xx]
            for dy in range(1, ny):
                acc += recv_y[g, dy - 1, xx].astype(F32)
            if o == 0:
                keep_2[half_z:nz, g] = acc
            else:
                send_2[1, g, o - 1] = acc.astype(BF16)
                second(1, g, o).start()

    def end_second(g):
        for part in range(2):
            own = slice(0, half_z) if part == 0 else slice(half_z, nz)
            acc = keep_2[own, g]
            whole(
                send_2.at[part, g], recv_2.at[part, g], s2_sem, r2_sem.at[part, g]
            ).wait_recv()
            for o in range(1, nx):
                acc += recv_2[part, g, o - 1].astype(F32)
            keep_2[own, g] = acc
            send_3[own, g] = acc.astype(BF16)

    ones = jnp.ones((16, 256), BF16)

    def val_norm(b):
        wide = val_v[b].astype(F32)
        sq = wide * wide
        high = sq.astype(BF16)
        low = (sq - high.astype(F32)).astype(BF16)
        dims = (((1,), (1,)), ((), ()))
        val_sq[b] = (
            lax.dot_general(ones, high, dims, preferred_element_type=F32)
            + lax.dot_general(ones, low, dims, preferred_element_type=F32)
        )[0:8]

    def norms(k):
        val_cross(k, 1).wait_recv()
        if 1 <= k <= ring_minus:
            val_cross(k, -1).wait_recv()
        for c in range(2):
            val_norm(depth(-k) * 2 + c)
            if 1 <= k <= ring_minus:
                val_norm(depth(k) * 2 + c)

    for g in range(groups):
        blocks = pl.ds(0, ex_n - 1)
        whole(send_a.at[g, blocks], recv_a.at[g, blocks], as_sem.at[g], ar_sem.at[g]).wait_recv()

        def gather(t, _, g=g):
            pair = recv_a[g, pl.ds(2 * t, 2)].astype(F32)
            place = pl.ds(pl.multiple_of(g * ex_n * 8 + t * 16, 16), 16)
            for h in range(2):
                lhs[place, h * 512 : (h + 1) * 512] = jnp.concatenate(
                    [pair[0, h * 8 : h * 8 + 8], pair[1, h * 8 : h * 8 + 8]], axis=0
                ).astype(BF16)
            return 0

        lax.fori_loop(0, ex_n // 2, gather, 0)
        if g == 0:
            pltpu.make_async_copy(proj_hbm, proj_v, proj_sem).wait()
        first = g * ny
        ahead = min(3, ny)
        lax.fori_loop(first, first + ahead, chunk, 0)

        def both(u, _, ahead=ahead):
            chunk(u, 0)
            pass_on(u - ahead)
            return 0

        lax.fori_loop(first + ahead, first + ny, both, 0)
        lax.fori_loop(first + ny - ahead, first + ny, pass_group, 0)
        if g >= 1:
            pass_second(g - 1)
        if 2 <= g + 2 <= ring_plus:
            val_point(g + 2)
            norms(g)
    done = min(groups, max(ring_plus - 1, 0))
    pass_second(groups - 1)
    for g in range(groups - 1):
        end_second(g)
    for k in range(max(groups + 2, 2), ring_plus + 1):
        val_point(k)
    for k in range(done, ring_plus + 1):
        norms(k)
    end_second(groups - 1)

    def third(o):
        return remote(
            send_3.at[depth(o)], recv_3.at[o - 1], s3_sem, r3_sem,
            ex, depth(o) * 2 + core,
        )

    for o in range(1, nz):
        third(o).start()

    for g in range(groups):
        whole(send_a.at[g, blocks], recv_a.at[g, blocks], as_sem.at[g], ar_sem.at[g]).wait_send()
    whole(prod.at[:, 0], recv_c, cs_sem, cr_sem.at[0]).wait_send()
    hops, crosses = val_v.at[pl.ds(0, nz - 1)], val_v.at[pl.ds(0, nz)]
    whole(hops, hops, vs_sem, vr_sem.at[0]).wait_send()
    whole(crosses, crosses, ws_sem, wr_sem.at[0]).wait_send()
    whole(send_x, recv_x, sx_sem, rx_sem.at[0, 0]).wait_send()
    whole(send_y, recv_y, sy_sem, ry_sem.at[0]).wait_send()
    whole(send_2, recv_2, s2_sem, r2_sem.at[0, 0]).wait_send()

    last = whole(send_3.at[pl.ds(0, nz - 1)], recv_3, s3_sem, r3_sem)
    last.wait_recv()
    acc = keep_2[z]
    for o in range(1, nz):
        acc += recv_3[o - 1].astype(F32)
    rows = groups * 8
    wide = jnp.concatenate(
        [
            jnp.concatenate([acc[g, l * 8 : (l + 1) * 8] for g in range(groups)], axis=0)
            for l in range(2)
        ],
        axis=1,
    )
    features = wide.astype(BF16)
    out_ref[0] = features.astype(F32)

    rounded = features.astype(F32)
    column = jnp.sum(rounded * rounded, axis=1, keepdims=True)
    diagonal = lax.broadcasted_iota(jnp.int32, (rows, 256), 0) == lax.broadcasted_iota(
        jnp.int32, (rows, 256), 1
    )
    feat_row = jnp.sum(jnp.where(diagonal, column, 0.0), axis=0, keepdims=True)
    padded = jnp.concatenate([rounded, jnp.zeros((8, 256), F32)], axis=0).astype(BF16)
    sub = lax.broadcasted_iota(jnp.int32, (8, 256), 0)

    def split(row):
        first = row.astype(BF16).astype(F32)
        second_ = (row - first).astype(BF16).astype(F32)
        return first, second_, row - first - second_

    feat_rows = split(feat_row)

    def dots_copy(o):
        to = plane(o // nx, o % nx)
        return remote(
            send_d.at[to], recv_d.at[o], ds_sem, dr_sem, to, par
        )

    for o in [*range(ex_n - 1, 0, -1), 0]:
        b = plane(o // nx, o % nx)
        part = lax.dot_general(
            padded, val_v[b], (((1,), (1,)), ((), ())), preferred_element_type=F32
        )
        extra = jnp.zeros((8, 256), F32)
        for k, row in enumerate((*split(val_sq[b]), *feat_rows)):
            extra = jnp.where(sub == k, row, extra)
        send_d[b] = jnp.concatenate([part[0:rows], extra], axis=0).astype(BF16)
        if o != 0:
            dots_copy(o).start()

    total = send_d[ex].astype(F32)
    every = whole(
        send_d.at[pl.ds(0, ex_n - 1)], recv_d.at[pl.ds(1, ex_n - 1)], ds_sem, dr_sem
    )
    every.wait_recv()
    for o in range(1, ex_n):
        total = total + recv_d[o].astype(F32)
    val_row = total[rows : rows + 1] + total[rows + 1 : rows + 2] + total[rows + 2 : rows + 3]
    feat_row = total[rows + 3 : rows + 4] + total[rows + 4 : rows + 5] + total[rows + 5 : rows + 6]
    feat_sq = jnp.sum(jnp.where(diagonal, feat_row, 0.0), axis=1, keepdims=True)
    factor = float(256 * ex_n) ** 0.5
    out_ref[1] = (
        factor * total[0:rows] * lax.rsqrt(feat_sq + 1e-06) * lax.rsqrt(val_row + 1e-06)
    )

    every.wait_send()
    last.wait_send()

def shards(ny, nx, nz, adapter_inputs, output_gradient, lengths, projection, validation):
    adapter_inputs = jnp.swapaxes(adapter_inputs, 1, 2)
    count, rank, tokens = adapter_inputs.shape
    width = output_gradient.shape[2]
    ex_n, par_n = ny * nx, nz * 2
    groups = count // 8
    vm, dma = pltpu.VMEM, pltpu.SemaphoreType.DMA
    half_z = nz // 2
    x_block, y_block = (half_z, 16, 128), (nx, half_z, 16, 128)
    scratch = [
        pltpu.SMEM(lengths.shape, jnp.int32),
        vm((count, rank, tokens), BF16),
        vm((count, tokens, width), BF16),
        vm(projection.shape, BF16),
        vm((par_n, 256, 256), BF16),
        vm((8 * ex_n * 8, 128), F32),
        vm((groups, ex_n, 16, 512), BF16),
        vm((groups, ex_n, 16, 512), BF16),
        vm((groups * ex_n * 8, 1024), BF16),
        vm((groups * ny, 2, nx, nz, 16, 128), F32),
        vm((groups * ny, nx, nz, 16, 128), F32),
        vm((groups, ny, nx - 1, *x_block), BF16),
        vm((groups, ny, nx - 1, *x_block), BF16),
        vm((groups, ny, *x_block), F32),
        vm((groups, ny - 1, *y_block), BF16),
        vm((groups, ny - 1, *y_block), BF16),
        vm((groups, *y_block), F32),
        vm((2, groups, nx - 1, *x_block), BF16),
        vm((2, groups, nx - 1, *x_block), BF16),
        vm((nz, groups, 16, 128), F32),
        vm((nz, groups, 16, 128), BF16),
        vm((nz - 1, groups, 16, 128), BF16),
        vm((par_n, 8, 256), F32),
        vm((ex_n, 32, 256), BF16),
        vm((ex_n, 32, 256), BF16),
        dma(()),
        dma((groups,)),
        dma((groups,)),
        dma(()),
        dma(()),
        dma((groups,)),
        dma((groups,)),
        dma(()),
        dma((nz,)),
        dma(()),
        dma((nz,)),
        dma(()),
        dma((groups * ny,)),
        dma(()),
        dma((groups, ny)),
        dma(()),
        dma((groups,)),
        dma(()),
        dma((2, groups)),
        dma(()),
        dma(()),
        dma(()),
        dma(()),
    ]
    anywhere = pl.BlockSpec(memory_space=pl.ANY)
    local = pl.BlockSpec(memory_space=pltpu.VMEM)
    out = pl.pallas_call(
        functools.partial(kernel, ny, nx, nz, groups, rank),
        out_shape=jax.ShapeDtypeStruct((2, count, 256), F32),
        in_specs=[anywhere, anywhere, anywhere, anywhere, anywhere],
        out_specs=local,
        scratch_shapes=scratch,
        compiler_params=pltpu.CompilerParams(
            collective_id=0, has_side_effects=True, vmem_limit_bytes=55091 * 1024
        ),
        cost_estimate=pl.CostEstimate(
            flops=4_000_000_000, bytes_accessed=13_000_000, transcendentals=0
        ),
    )(adapter_inputs, output_gradient, lengths, projection, validation)
    return out[0].astype(BF16), out[1]


def solution(mesh):
    ex_n, par_n = mesh.shape["ex"], mesh.shape["par"]
    nx = 1
    while nx * nx < ex_n:
        nx *= 2
    in_specs = (
        P("ex", None, None),
        P("ex", None, "par"),
        P("ex"),
        P(("par", "ex"), None),
        P("par", "ex"),
    )
    out_specs = (P("par", "ex"), P("par", "ex"))
    return jax.shard_map(
        functools.partial(shards, ex_n // nx, nx, par_n // 2),
        mesh=mesh,
        in_specs=in_specs,
        out_specs=out_specs,
        check_vma=False,
    )
```

```python
import functools

import jax
import jax.numpy as jnp
from jax import lax
from jax.experimental import pallas as pl
from jax.experimental.pallas import tpu as pltpu
from jax.sharding import PartitionSpec as P

MESH = pl.DeviceIdType.MESH
F32 = jnp.float32
BF16 = jnp.bfloat16


def kernel(
    ny, nx, nz, groups, rank,
    ai_hbm, og_hbm, len_hbm, proj_hbm, val_hbm,
    out_ref,
    len_ref, ai_v, og_v, proj_v, val_v, stage_v, send_a, recv_a, lhs, prod, recv_c,
    send_x, recv_x, keep_x, send_y, recv_y, keep_y, send_2, recv_2, keep_2,
    send_3, recv_3, val_sq, send_d, recv_d,
    len_sem, ai_sem, og_sem, proj_sem, val_sem,
    as_sem, ar_sem, vs_sem, vr_sem, ws_sem, wr_sem, cs_sem, cr_sem,
    sx_sem, rx_sem, sy_sem, ry_sem, s2_sem, r2_sem, s3_sem, r3_sem, ds_sem, dr_sem,
):
    ex_n = ny * nx
    ex = lax.axis_index("ex")
    par = lax.axis_index("par")
    y, x = lax.div(ex, nx), lax.rem(ex, nx)
    z, core = lax.div(par, 2), lax.rem(par, 2)
    tokens = ai_v.shape[2]
    half_z = nz // 2

    def plane(oy, ox):
        return lax.rem(y + oy, ny) * nx + lax.rem(x + ox, nx)

    def depth(oz):
        return lax.rem(z + oz + nz, nz)

    def remote(src, dst, ssem, rsem, to_ex, to_par):
        return pltpu.make_async_remote_copy(
            src_ref=src, dst_ref=dst, send_sem=ssem, recv_sem=rsem,
            device_id=(to_ex, to_par), device_id_type=MESH,
        )

    def load(g):
        rows = pl.ds(g * 8, 8)
        pltpu.make_async_copy(og_hbm.at[rows], og_v.at[rows], og_sem.at[g]).start()
        pltpu.make_async_copy(ai_hbm.at[rows], ai_v.at[rows], ai_sem.at[g]).start()

    load(0)
    len_copy = pltpu.make_async_copy(len_hbm, len_ref, len_sem)
    len_copy.start()

    barrier = pltpu.get_barrier_semaphore()

    def greet(to_ex, to_par):
        pl.semaphore_signal(barrier, inc=1, device_id=(to_ex, to_par), device_id_type=MESH)

    for o in range(1, ex_n):
        greet(plane(o // nx, o % nx), par)

    for o in range(1, nz):
        greet(ex, depth(o) * 2 + core)
    greet(ex, z * 2 + 1 - core)

    def whole(src, dst, ssem, rsem):
        return remote(src, dst, ssem, rsem, ex, z * 2 + 1 - core)

    for g in range(1, groups):
        load(g)
    val_copy = pltpu.make_async_copy(val_hbm, val_v.at[par], val_sem)
    val_copy.start()

    def proj_copy(s, q):
        return pltpu.make_async_copy(
            proj_hbm.at[pl.ds((q * 8 + s) * rank, rank)],
            proj_v.at[pl.ds(s * 2 * rank + q * rank, rank)],
            proj_sem,
        )

    ring_plus, ring_minus = nz // 2, (nz - 1) // 2

    def val_hop(k, sign):
        slot = depth(-sign * (k - 1)) * 2 + core
        sem = k if sign > 0 else ring_plus + k
        return remote(
            val_v.at[slot], val_v.at[slot], vs_sem, vr_sem.at[sem], ex, depth(sign) * 2 + core
        )

    def val_cross(k, sign):
        slot = depth(-sign * k) * 2 + core
        sem = k if sign > 0 else ring_plus + k
        return remote(
            val_v.at[slot], val_v.at[slot], ws_sem, wr_sem.at[sem], ex, z * 2 + 1 - core
        )

    def val_point(k):
        if k == 0:
            val_copy.wait()
            val_cross(0, 1).start()
        else:
            if k <= ring_plus:
                val_hop(k, 1).wait_recv()
                val_cross(k, 1).start()
            if k <= ring_minus:
                val_hop(k, -1).wait_recv()
                val_cross(k, -1).start()
        if k + 1 <= ring_plus:
            val_hop(k + 1, 1).start()
        if k + 1 <= ring_minus:
            val_hop(k + 1, -1).start()

    lane = lax.broadcasted_iota(jnp.int32, (ex_n, 8, 128), 2)

    def a2a(g, o):
        to = plane(o // nx, o % nx)
        return remote(
            send_a.at[g, to], recv_a.at[g, ex], as_sem.at[g], ar_sem.at[g], to, par
        )

    for g in range(groups):
        rows = pl.ds(g * 8, 8)
        pltpu.make_async_copy(ai_hbm.at[rows], ai_v.at[rows], ai_sem.at[g]).wait()
        pltpu.make_async_copy(og_hbm.at[rows], og_v.at[rows], og_sem.at[g]).wait()

        def gradient(e, _, g=g):
            m = g * 8 + e
            live = lax.broadcasted_iota(jnp.int32, (rank, tokens), 1) < len_ref[m]
            acts = jnp.where(live, ai_v[m].astype(F32), 0.0).astype(BF16)
            out = lax.dot_general(
                og_v[m], jnp.concatenate([acts, acts], axis=0),
                (((0,), (1,)), ((), ())), preferred_element_type=F32,
            )
            out = out.reshape(ex_n, 2, 8, 2 * rank)
            both = jnp.where(lane < rank, out[:, 0], out[:, 1])
            stage_v[pl.ds(pl.multiple_of(e * ex_n * 8, ex_n * 8), ex_n * 8), :] = both.reshape(
                ex_n * 8, 2 * rank
            )
            return 0

        if g == 0:
            len_copy.wait()
        lax.fori_loop(0, 8, gradient, 0, unroll=4)

        def pack(j, _, g=g):
            for q in range(4):
                low = stage_v[pl.ds(j * 8 + q, 8, stride=ex_n * 8), :]
                high = stage_v[pl.ds(j * 8 + q + 4, 8, stride=ex_n * 8), :]
                send_a[g, j, :, q * 128 : (q + 1) * 128] = jnp.concatenate(
                    [low, high], axis=0
                ).astype(BF16)
            return 0

        lax.fori_loop(0, ex_n, pack, 0, unroll=4)
        recv_a[g, ex] = send_a[g, ex]
        if g == 0:
            pl.semaphore_wait(barrier, ex_n - 1 + nz - 1 + 1)

        for o in range(1, ex_n):
            a2a(g, o).start()
        if g == 0:
            for s in range(8):
                for q in range(2):
                    proj_copy(s, q).start()
            val_point(0)
        if g == groups - 1:
            val_point(1)

    def row_of(u):
        return lax.rem(lax.rem(u, ny) + 1, ny)

    def core_copy(u):
        return remote(
            prod.at[u, 1 - core], recv_c.at[u], cs_sem, cr_sem.at[u], ex, z * 2 + 1 - core
        )

    def first_x(g, dy, dx):
        return remote(
            send_x.at[g, dy, dx - 1], recv_x.at[g, dy, dx - 1],
            sx_sem, rx_sem.at[g, dy], plane(0, dx), par,
        )

    def first_y(g, dy):
        return remote(
            send_y.at[g, dy - 1], recv_y.at[g, dy - 1],
            sy_sem, ry_sem.at[g], plane(dy, 0), par,
        )

    def pass_on(u):
        g, dy = lax.div(u, ny), row_of(u)
        core_copy(u).wait_recv()
        for dx in [*range(1, nx), 0]:
            xx = lax.rem(x + dx, nx)
            total = prod[u, core, xx, 0:half_z] + recv_c[u, xx, 0:half_z]
            if dx == 0:
                keep_x[g, dy] = total
            else:
                send_x[g, dy, dx - 1] = total.astype(BF16)
                first_x(g, dy, dx).start()

        @pl.when(dy == 0)
        def _():
            for xx in range(nx):
                keep_y[g, xx] = prod[u, core, xx, half_z:nz] + recv_c[u, xx, half_z:nz]

        @pl.when(dy != 0)
        def _():
            for xx in range(nx):
                send_y[g, dy - 1, xx] = (
                    prod[u, core, xx, half_z:nz] + recv_c[u, xx, half_z:nz]
                ).astype(BF16)
            first_y(g, dy).start()

    def chunk(u, _):
        g = lax.div(u, ny)
        yy = lax.rem(y + row_of(u), ny)
        left = lhs[pl.ds(pl.multiple_of(g * ex_n * 8, 16), ex_n * 8), :]
        for xx in range(nx):
            out = jnp.dot(
                left, proj_v[:, pl.ds(pl.multiple_of((yy * nx + xx) * 256, 256), 256)],
                preferred_element_type=F32,
            )
            for l in range(2):
                part = out[:, l * 128 : (l + 1) * 128].reshape(nz, 2, 8, 128)
                for c in range(2):
                    prod[u, c, xx, :, l * 8 : (l + 1) * 8, :] = part[:, c]
        core_copy(u).start()
        return 0

    def pass_group(u, _):
        pass_on(u)
        return 0

    def second(part, g, o):
        to = plane(o, 0) if part == 0 else plane(0, o)
        return remote(
            send_2.at[part, g, o - 1], recv_2.at[part, g, o - 1],
            s2_sem, r2_sem.at[part, g], to, par,
        )

    def pass_second(g):
        whole(send_y.at[g], recv_y.at[g], sy_sem, ry_sem.at[g]).wait_recv()
        for o in [*range(1, nx), 0]:
            whole(send_x.at[g, o], recv_x.at[g, o], sx_sem, rx_sem.at[g, o]).wait_recv()
            acc = keep_x[g, o]
            for dx in range(1, nx):
                acc += recv_x[g, o, dx - 1].astype(F32)
            if o == 0:
                keep_2[0:half_z, g] = acc
            else:
                send_2[0, g, o - 1] = acc.astype(BF16)
                second(0, g, o).start()
            xx = lax.rem(x + o, nx)
            acc = keep_y[g, xx]
            for dy in range(1, ny):
                acc += recv_y[g, dy - 1, xx].astype(F32)
            if o == 0:
                keep_2[half_z:nz, g] = acc
            else:
                send_2[1, g, o - 1] = acc.astype(BF16)
                second(1, g, o).start()

    def end_second(g):
        for part in range(2):
            own = slice(0, half_z) if part == 0 else slice(half_z, nz)
            acc = keep_2[own, g]
            whole(
                send_2.at[part, g], recv_2.at[part, g], s2_sem, r2_sem.at[part, g]
            ).wait_recv()
            for o in range(1, nx):
                acc += recv_2[part, g, o - 1].astype(F32)
            keep_2[own, g] = acc
            send_3[own, g] = acc.astype(BF16)

    ones = jnp.ones((16, 256), BF16)

    def val_norm(b):
        wide = val_v[b].astype(F32)
        sq = wide * wide
        high = sq.astype(BF16)
        low = (sq - high.astype(F32)).astype(BF16)
        dims = (((1,), (1,)), ((), ()))
        val_sq[b] = (
            lax.dot_general(ones, high, dims, preferred_element_type=F32)
            + lax.dot_general(ones, low, dims, preferred_element_type=F32)
        )[0:8]

    def norms(k):
        val_cross(k, 1).wait_recv()
        if 1 <= k <= ring_minus:
            val_cross(k, -1).wait_recv()
        for c in range(2):
            val_norm(depth(-k) * 2 + c)
            if 1 <= k <= ring_minus:
                val_norm(depth(k) * 2 + c)

    for g in range(groups):
        blocks = pl.ds(0, ex_n - 1)
        whole(send_a.at[g, blocks], recv_a.at[g, blocks], as_sem.at[g], ar_sem.at[g]).wait_recv()

        def gather(t, _, g=g):
            pair = recv_a[g, pl.ds(2 * t, 2)].astype(F32)
            place = pl.ds(pl.multiple_of(g * ex_n * 8 + t * 16, 16), 16)
            for h in range(2):
                lhs[place, h * 512 : (h + 1) * 512] = jnp.concatenate(
                    [pair[0, h * 8 : h * 8 + 8], pair[1, h * 8 : h * 8 + 8]], axis=0
                ).astype(BF16)
            return 0

        lax.fori_loop(0, ex_n // 2, gather, 0)
        if g == 0:
            pltpu.make_async_copy(proj_hbm, proj_v, proj_sem).wait()
        first = g * ny
        ahead = min(3, ny)
        lax.fori_loop(first, first + ahead, chunk, 0)

        def both(u, _, ahead=ahead):
            chunk(u, 0)
            pass_on(u - ahead)
            return 0

        lax.fori_loop(first + ahead, first + ny, both, 0)
        lax.fori_loop(first + ny - ahead, first + ny, pass_group, 0)
        if 2 <= g + 2 <= ring_plus:
            val_point(g + 2)
            norms(g)
    done = min(groups, max(ring_plus - 1, 0))
    for g in range(groups):
        pass_second(g)
    for g in range(groups - 1):
        end_second(g)
    for k in range(max(groups + 2, 2), ring_plus + 1):
        val_point(k)
    for k in range(done, ring_plus + 1):
        norms(k)
    end_second(groups - 1)

    def third(o):
        return remote(
            send_3.at[depth(o)], recv_3.at[o - 1], s3_sem, r3_sem,
            ex, depth(o) * 2 + core,
        )

    for o in range(1, nz):
        third(o).start()

    for g in range(groups):
        whole(send_a.at[g, blocks], recv_a.at[g, blocks], as_sem.at[g], ar_sem.at[g]).wait_send()
    whole(prod.at[:, 0], recv_c, cs_sem, cr_sem.at[0]).wait_send()
    hops, crosses = val_v.at[pl.ds(0, nz - 1)], val_v.at[pl.ds(0, nz)]
    whole(hops, hops, vs_sem, vr_sem.at[0]).wait_send()
    whole(crosses, crosses, ws_sem, wr_sem.at[0]).wait_send()
    whole(send_x, recv_x, sx_sem, rx_sem.at[0, 0]).wait_send()
    whole(send_y, recv_y, sy_sem, ry_sem.at[0]).wait_send()
    whole(send_2, recv_2, s2_sem, r2_sem.at[0, 0]).wait_send()

    last = whole(send_3.at[pl.ds(0, nz - 1)], recv_3, s3_sem, r3_sem)
    last.wait_recv()
    acc = keep_2[z]
    for o in range(1, nz):
        acc += recv_3[o - 1].astype(F32)
    rows = groups * 8
    wide = jnp.concatenate(
        [
            jnp.concatenate([acc[g, l * 8 : (l + 1) * 8] for g in range(groups)], axis=0)
            for l in range(2)
        ],
        axis=1,
    )
    features = wide.astype(BF16)
    out_ref[0] = features.astype(F32)

    rounded = features.astype(F32)
    column = jnp.sum(rounded * rounded, axis=1, keepdims=True)
    diagonal = lax.broadcasted_iota(jnp.int32, (rows, 256), 0) == lax.broadcasted_iota(
        jnp.int32, (rows, 256), 1
    )
    feat_row = jnp.sum(jnp.where(diagonal, column, 0.0), axis=0, keepdims=True)
    padded = jnp.concatenate([rounded, jnp.zeros((8, 256), F32)], axis=0).astype(BF16)
    sub = lax.broadcasted_iota(jnp.int32, (8, 256), 0)

    def split(row):
        first = row.astype(BF16).astype(F32)
        second_ = (row - first).astype(BF16).astype(F32)
        return first, second_, row - first - second_

    feat_rows = split(feat_row)

    def dots_copy(o):
        to = plane(o // nx, o % nx)
        return remote(
            send_d.at[to], recv_d.at[o], ds_sem, dr_sem, to, par
        )

    for o in [*range(ex_n - 1, 0, -1), 0]:
        b = plane(o // nx, o % nx)
        part = lax.dot_general(
            padded, val_v[b], (((1,), (1,)), ((), ())), preferred_element_type=F32
        )
        extra = jnp.zeros((8, 256), F32)
        for k, row in enumerate((*split(val_sq[b]), *feat_rows)):
            extra = jnp.where(sub == k, row, extra)
        send_d[b] = jnp.concatenate([part[0:rows], extra], axis=0).astype(BF16)
        if o != 0:
            dots_copy(o).start()

    total = send_d[ex].astype(F32)
    every = whole(
        send_d.at[pl.ds(0, ex_n - 1)], recv_d.at[pl.ds(1, ex_n - 1)], ds_sem, dr_sem
    )
    every.wait_recv()
    for o in range(1, ex_n):
        total = total + recv_d[o].astype(F32)
    val_row = total[rows : rows + 1] + total[rows + 1 : rows + 2] + total[rows + 2 : rows + 3]
    feat_row = total[rows + 3 : rows + 4] + total[rows + 4 : rows + 5] + total[rows + 5 : rows + 6]
    feat_sq = jnp.sum(jnp.where(diagonal, feat_row, 0.0), axis=1, keepdims=True)
    factor = float(256 * ex_n) ** 0.5
    out_ref[1] = (
        factor * total[0:rows] * lax.rsqrt(feat_sq + 1e-06) * lax.rsqrt(val_row + 1e-06)
    )

    every.wait_send()
    last.wait_send()

def shards(ny, nx, nz, adapter_inputs, output_gradient, lengths, projection, validation):
    adapter_inputs = jnp.swapaxes(adapter_inputs, 1, 2)
    count, rank, tokens = adapter_inputs.shape
    width = output_gradient.shape[2]
    ex_n, par_n = ny * nx, nz * 2
    groups = count // 8
    vm, dma = pltpu.VMEM, pltpu.SemaphoreType.DMA
    half_z = nz // 2
    x_block, y_block = (half_z, 16, 128), (nx, half_z, 16, 128)
    scratch = [
        pltpu.SMEM(lengths.shape, jnp.int32),
        vm((count, rank, tokens), BF16),
        vm((count, tokens, width), BF16),
        vm(projection.shape, BF16),
        vm((par_n, 256, 256), BF16),
        vm((8 * ex_n * 8, 128), F32),
        vm((groups, ex_n, 16, 512), BF16),
        vm((groups, ex_n, 16, 512), BF16),
        vm((groups * ex_n * 8, 1024), BF16),
        vm((groups * ny, 2, nx, nz, 16, 128), F32),
        vm((groups * ny, nx, nz, 16, 128), F32),
        vm((groups, ny, nx - 1, *x_block), BF16),
        vm((groups, ny, nx - 1, *x_block), BF16),
        vm((groups, ny, *x_block), F32),
        vm((groups, ny - 1, *y_block), BF16),
        vm((groups, ny - 1, *y_block), BF16),
        vm((groups, *y_block), F32),
        vm((2, groups, nx - 1, *x_block), BF16),
        vm((2, groups, nx - 1, *x_block), BF16),
        vm((nz, groups, 16, 128), F32),
        vm((nz, groups, 16, 128), BF16),
        vm((nz - 1, groups, 16, 128), BF16),
        vm((par_n, 8, 256), F32),
        vm((ex_n, 32, 256), BF16),
        vm((ex_n, 32, 256), BF16),
        dma(()),
        dma((groups,)),
        dma((groups,)),
        dma(()),
        dma(()),
        dma((groups,)),
        dma((groups,)),
        dma(()),
        dma((nz,)),
        dma(()),
        dma((nz,)),
        dma(()),
        dma((groups * ny,)),
        dma(()),
        dma((groups, ny)),
        dma(()),
        dma((groups,)),
        dma(()),
        dma((2, groups)),
        dma(()),
        dma(()),
        dma(()),
        dma(()),
    ]
    anywhere = pl.BlockSpec(memory_space=pl.ANY)
    local = pl.BlockSpec(memory_space=pltpu.VMEM)
    out = pl.pallas_call(
        functools.partial(kernel, ny, nx, nz, groups, rank),
        out_shape=jax.ShapeDtypeStruct((2, count, 256), F32),
        in_specs=[anywhere, anywhere, anywhere, anywhere, anywhere],
        out_specs=local,
        scratch_shapes=scratch,
        compiler_params=pltpu.CompilerParams(
            collective_id=0, has_side_effects=True, vmem_limit_bytes=55091 * 1024
        ),
        cost_estimate=pl.CostEstimate(
            flops=4_000_000_000, bytes_accessed=13_000_000, transcendentals=0
        ),
    )(adapter_inputs, output_gradient, lengths, projection, validation)
    return out[0].astype(BF16), out[1]


def solution(mesh):
    ex_n, par_n = mesh.shape["ex"], mesh.shape["par"]
    nx = 1
    while nx * nx < ex_n:
        nx *= 2
    in_specs = (
        P("ex", None, None),
        P("ex", None, "par"),
        P("ex"),
        P(("par", "ex"), None),
        P("par", "ex"),
    )
    out_specs = (P("par", "ex"), P("par", "ex"))
    return jax.shard_map(
        functools.partial(shards, ex_n // nx, nx, par_n // 2),
        mesh=mesh,
        in_specs=in_specs,
        out_specs=out_specs,
        check_vma=False,
    )
```

```python
import functools

import jax
import jax.numpy as jnp
from jax import lax
from jax.experimental import pallas as pl
from jax.experimental.pallas import tpu as pltpu
from jax.sharding import PartitionSpec as P

MESH = pl.DeviceIdType.MESH
F32 = jnp.float32
BF16 = jnp.bfloat16


def kernel(
    ny, nx, nz, groups, rank,
    ai_hbm, og_hbm, len_hbm, proj_hbm, val_hbm,
    out_ref,
    len_ref, ai_v, og_v, proj_v, val_v, stage_v, send_a, recv_a, lhs, prod, recv_c,
    send_x, recv_x, keep_x, send_y, recv_y, keep_y, send_2, recv_2, keep_2,
    send_3, recv_3, val_sq, send_d, recv_d,
    len_sem, ai_sem, og_sem, proj_sem, val_sem,
    as_sem, ar_sem, vs_sem, vr_sem, ws_sem, wr_sem, cs_sem, cr_sem,
    sx_sem, rx_sem, sy_sem, ry_sem, s2_sem, r2_sem, s3_sem, r3_sem, ds_sem, dr_sem,
):
    ex_n = ny * nx
    ex = lax.axis_index("ex")
    par = lax.axis_index("par")
    y, x = lax.div(ex, nx), lax.rem(ex, nx)
    z, core = lax.div(par, 2), lax.rem(par, 2)
    tokens = ai_v.shape[2]
    half_z = nz // 2

    def plane(oy, ox):
        return lax.rem(y + oy, ny) * nx + lax.rem(x + ox, nx)

    def depth(oz):
        return lax.rem(z + oz + nz, nz)

    def remote(src, dst, ssem, rsem, to_ex, to_par):
        return pltpu.make_async_remote_copy(
            src_ref=src, dst_ref=dst, send_sem=ssem, recv_sem=rsem,
            device_id=(to_ex, to_par), device_id_type=MESH,
        )

    def load(g):
        rows = pl.ds(g * 8, 8)
        pltpu.make_async_copy(og_hbm.at[rows], og_v.at[rows], og_sem.at[g]).start()
        pltpu.make_async_copy(ai_hbm.at[rows], ai_v.at[rows], ai_sem.at[g]).start()

    load(0)
    len_copy = pltpu.make_async_copy(len_hbm, len_ref, len_sem)
    len_copy.start()

    barrier = pltpu.get_barrier_semaphore()

    def greet(to_ex, to_par):
        pl.semaphore_signal(barrier, inc=1, device_id=(to_ex, to_par), device_id_type=MESH)

    for o in range(1, ex_n):
        greet(plane(o // nx, o % nx), par)

    for o in sorted({1, nz - 1}):
        greet(ex, depth(o) * 2 + core)
    greet(ex, z * 2 + 1 - core)

    def whole(src, dst, ssem, rsem):
        return remote(src, dst, ssem, rsem, ex, z * 2 + 1 - core)

    for g in range(1, groups):
        load(g)
    val_copy = pltpu.make_async_copy(val_hbm, val_v.at[par], val_sem)
    val_copy.start()

    def proj_copy(s, q):
        return pltpu.make_async_copy(
            proj_hbm.at[pl.ds((q * 8 + s) * rank, rank)],
            proj_v.at[pl.ds(s * 2 * rank + q * rank, rank)],
            proj_sem,
        )

    ring_plus, ring_minus = nz // 2, (nz - 1) // 2

    def val_hop(k, sign):
        slot = depth(-sign * (k - 1)) * 2 + core
        sem = k if sign > 0 else ring_plus + k
        return remote(
            val_v.at[slot], val_v.at[slot], vs_sem, vr_sem.at[sem], ex, depth(sign) * 2 + core
        )

    def val_cross(k, sign):
        slot = depth(-sign * k) * 2 + core
        sem = k if sign > 0 else ring_plus + k
        return remote(
            val_v.at[slot], val_v.at[slot], ws_sem, wr_sem.at[sem], ex, z * 2 + 1 - core
        )

    def val_point(k):
        if k == 0:
            val_copy.wait()
            val_cross(0, 1).start()
        else:
            if k <= ring_plus:
                val_hop(k, 1).wait_recv()
                val_cross(k, 1).start()
            if k <= ring_minus:
                val_hop(k, -1).wait_recv()
                val_cross(k, -1).start()
        if k + 1 <= ring_plus:
            val_hop(k + 1, 1).start()
        if k + 1 <= ring_minus:
            val_hop(k + 1, -1).start()

    lane = lax.broadcasted_iota(jnp.int32, (ex_n, 8, 128), 2)

    def a2a(g, o):
        to = plane(o // nx, o % nx)
        return remote(
            send_a.at[g, to], recv_a.at[g, ex], as_sem.at[g], ar_sem.at[g], to, par
        )

    for g in range(groups):
        rows = pl.ds(g * 8, 8)
        pltpu.make_async_copy(ai_hbm.at[rows], ai_v.at[rows], ai_sem.at[g]).wait()
        pltpu.make_async_copy(og_hbm.at[rows], og_v.at[rows], og_sem.at[g]).wait()

        def gradient(e, _, g=g):
            m = g * 8 + e
            live = lax.broadcasted_iota(jnp.int32, (rank, tokens), 1) < len_ref[m]
            acts = jnp.where(live, ai_v[m].astype(F32), 0.0).astype(BF16)
            out = lax.dot_general(
                og_v[m], jnp.concatenate([acts, acts], axis=0),
                (((0,), (1,)), ((), ())), preferred_element_type=F32,
            )
            out = out.reshape(ex_n, 2, 8, 2 * rank)
            both = jnp.where(lane < rank, out[:, 0], out[:, 1])
            stage_v[pl.ds(pl.multiple_of(e * ex_n * 8, ex_n * 8), ex_n * 8), :] = both.reshape(
                ex_n * 8, 2 * rank
            )
            return 0

        if g == 0:
            len_copy.wait()
        lax.fori_loop(0, 8, gradient, 0, unroll=4)

        def pack(j, _, g=g):
            for q in range(4):
                low = stage_v[pl.ds(j * 8 + q, 8, stride=ex_n * 8), :]
                high = stage_v[pl.ds(j * 8 + q + 4, 8, stride=ex_n * 8), :]
                send_a[g, j, :, q * 128 : (q + 1) * 128] = jnp.concatenate(
                    [low, high], axis=0
                ).astype(BF16)
            return 0

        lax.fori_loop(0, ex_n, pack, 0, unroll=4)
        recv_a[g, ex] = send_a[g, ex]
        if g == 0:
            pl.semaphore_wait(barrier, ex_n - 1 + len({1, nz - 1}) + 1)

        for o in range(1, ex_n):
            a2a(g, o).start()
        if g == 0:
            for s in range(8):
                for q in range(2):
                    proj_copy(s, q).start()
            val_point(0)
        if g == groups - 1:
            val_point(1)

    def row_of(u):
        return lax.rem(lax.rem(u, ny) + 1, ny)

    def core_copy(u):
        return remote(
            prod.at[u, 1 - core], recv_c.at[u], cs_sem, cr_sem.at[u], ex, z * 2 + 1 - core
        )

    def first_x(g, dy, dx):
        return remote(
            send_x.at[g, dy, dx - 1], recv_x.at[g, dy, dx - 1],
            sx_sem, rx_sem.at[g, dy], plane(0, dx), par,
        )

    def first_y(g, dy):
        return remote(
            send_y.at[g, dy - 1], recv_y.at[g, dy - 1],
            sy_sem, ry_sem.at[g], plane(dy, 0), par,
        )

    def pass_on(u):
        g, dy = lax.div(u, ny), row_of(u)
        core_copy(u).wait_recv()
        for dx in [*range(1, nx), 0]:
            xx = lax.rem(x + dx, nx)
            total = prod[u, core, xx, 0:half_z] + recv_c[u, xx, 0:half_z]
            if dx == 0:
                keep_x[g, dy] = total
            else:
                send_x[g, dy, dx - 1] = total.astype(BF16)
                first_x(g, dy, dx).start()

        @pl.when(dy == 0)
        def _():
            for xx in range(nx):
                keep_y[g, xx] = prod[u, core, xx, half_z:nz] + recv_c[u, xx, half_z:nz]

        @pl.when(dy != 0)
        def _():
            for xx in range(nx):
                send_y[g, dy - 1, xx] = (
                    prod[u, core, xx, half_z:nz] + recv_c[u, xx, half_z:nz]
                ).astype(BF16)
            first_y(g, dy).start()

    def chunk(u, _):
        g = lax.div(u, ny)
        yy = lax.rem(y + row_of(u), ny)
        left = lhs[pl.ds(pl.multiple_of(g * ex_n * 8, 16), ex_n * 8), :]
        for xx in range(nx):
            out = jnp.dot(
                left, proj_v[:, pl.ds(pl.multiple_of((yy * nx + xx) * 256, 256), 256)],
                preferred_element_type=F32,
            )
            for l in range(2):
                part = out[:, l * 128 : (l + 1) * 128].reshape(nz, 2, 8, 128)
                for c in range(2):
                    prod[u, c, xx, :, l * 8 : (l + 1) * 8, :] = part[:, c]
        core_copy(u).start()
        return 0

    def pass_group(u, _):
        pass_on(u)
        return 0

    def second(part, g, o):
        to = plane(o, 0) if part == 0 else plane(0, o)
        return remote(
            send_2.at[part, g, o - 1], recv_2.at[part, g, o - 1],
            s2_sem, r2_sem.at[part, g], to, par,
        )

    def pass_second(g):
        whole(send_y.at[g], recv_y.at[g], sy_sem, ry_sem.at[g]).wait_recv()
        for o in [*range(1, nx), 0]:
            whole(send_x.at[g, o], recv_x.at[g, o], sx_sem, rx_sem.at[g, o]).wait_recv()
            acc = keep_x[g, o]
            for dx in range(1, nx):
                acc += recv_x[g, o, dx - 1].astype(F32)
            if o == 0:
                keep_2[0:half_z, g] = acc
            else:
                send_2[0, g, o - 1] = acc.astype(BF16)
                second(0, g, o).start()
            xx = lax.rem(x + o, nx)
            acc = keep_y[g, xx]
            for dy in range(1, ny):
                acc += recv_y[g, dy - 1, xx].astype(F32)
            if o == 0:
                keep_2[half_z:nz, g] = acc
            else:
                send_2[1, g, o - 1] = acc.astype(BF16)
                second(1, g, o).start()

    def end_second(g):
        for part in range(2):
            own = slice(0, half_z) if part == 0 else slice(half_z, nz)
            acc = keep_2[own, g]
            whole(
                send_2.at[part, g], recv_2.at[part, g], s2_sem, r2_sem.at[part, g]
            ).wait_recv()
            for o in range(1, nx):
                acc += recv_2[part, g, o - 1].astype(F32)
            keep_2[own, g] = acc
            send_3[own, g] = acc.astype(BF16)

    ones = jnp.ones((16, 256), BF16)

    def val_norm(b):
        wide = val_v[b].astype(F32)
        sq = wide * wide
        high = sq.astype(BF16)
        low = (sq - high.astype(F32)).astype(BF16)
        dims = (((1,), (1,)), ((), ()))
        val_sq[b] = (
            lax.dot_general(ones, high, dims, preferred_element_type=F32)
            + lax.dot_general(ones, low, dims, preferred_element_type=F32)
        )[0:8]

    def norms(k):
        val_cross(k, 1).wait_recv()
        if 1 <= k <= ring_minus:
            val_cross(k, -1).wait_recv()
        for c in range(2):
            val_norm(depth(-k) * 2 + c)
            if 1 <= k <= ring_minus:
                val_norm(depth(k) * 2 + c)

    for g in range(groups):
        blocks = pl.ds(0, ex_n - 1)
        whole(send_a.at[g, blocks], recv_a.at[g, blocks], as_sem.at[g], ar_sem.at[g]).wait_recv()

        def gather(t, _, g=g):
            pair = recv_a[g, pl.ds(2 * t, 2)].astype(F32)
            place = pl.ds(pl.multiple_of(g * ex_n * 8 + t * 16, 16), 16)
            for h in range(2):
                lhs[place, h * 512 : (h + 1) * 512] = jnp.concatenate(
                    [pair[0, h * 8 : h * 8 + 8], pair[1, h * 8 : h * 8 + 8]], axis=0
                ).astype(BF16)
            return 0

        lax.fori_loop(0, ex_n // 2, gather, 0)
        if g == 0:
            pltpu.make_async_copy(proj_hbm, proj_v, proj_sem).wait()
        first = g * ny
        ahead = min(3, ny)
        lax.fori_loop(first, first + ahead, chunk, 0)

        def both(u, _, ahead=ahead):
            chunk(u, 0)
            pass_on(u - ahead)
            return 0

        lax.fori_loop(first + ahead, first + ny, both, 0)
        lax.fori_loop(first + ny - ahead, first + ny, pass_group, 0)
        if 2 <= g + 2 <= ring_plus:
            val_point(g + 2)
            norms(g)
    done = min(groups, max(ring_plus - 1, 0))
    for g in range(groups):
        pass_second(g)
    for g in range(groups - 1):
        end_second(g)
    for k in range(max(groups + 2, 2), ring_plus + 1):
        val_point(k)
    for k in range(done, ring_plus + 1):
        norms(k)
    end_second(groups - 1)

    def third(o):
        return remote(
            send_3.at[depth(o)], recv_3.at[o - 1], s3_sem, r3_sem,
            ex, depth(o) * 2 + core,
        )

    for o in range(1, nz):
        third(o).start()

    for g in range(groups):
        whole(send_a.at[g, blocks], recv_a.at[g, blocks], as_sem.at[g], ar_sem.at[g]).wait_send()
    whole(prod.at[:, 0], recv_c, cs_sem, cr_sem.at[0]).wait_send()
    hops, crosses = val_v.at[pl.ds(0, nz - 1)], val_v.at[pl.ds(0, nz)]
    whole(hops, hops, vs_sem, vr_sem.at[0]).wait_send()
    whole(crosses, crosses, ws_sem, wr_sem.at[0]).wait_send()
    whole(send_x, recv_x, sx_sem, rx_sem.at[0, 0]).wait_send()
    whole(send_y, recv_y, sy_sem, ry_sem.at[0]).wait_send()
    whole(send_2, recv_2, s2_sem, r2_sem.at[0, 0]).wait_send()

    last = whole(send_3.at[pl.ds(0, nz - 1)], recv_3, s3_sem, r3_sem)
    last.wait_recv()
    acc = keep_2[z]
    for o in range(1, nz):
        acc += recv_3[o - 1].astype(F32)
    rows = groups * 8
    wide = jnp.concatenate(
        [
            jnp.concatenate([acc[g, l * 8 : (l + 1) * 8] for g in range(groups)], axis=0)
            for l in range(2)
        ],
        axis=1,
    )
    features = wide.astype(BF16)
    out_ref[0] = features.astype(F32)

    rounded = features.astype(F32)
    column = jnp.sum(rounded * rounded, axis=1, keepdims=True)
    diagonal = lax.broadcasted_iota(jnp.int32, (rows, 256), 0) == lax.broadcasted_iota(
        jnp.int32, (rows, 256), 1
    )
    feat_row = jnp.sum(jnp.where(diagonal, column, 0.0), axis=0, keepdims=True)
    padded = jnp.concatenate([rounded, jnp.zeros((8, 256), F32)], axis=0).astype(BF16)
    sub = lax.broadcasted_iota(jnp.int32, (8, 256), 0)

    def split(row):
        first = row.astype(BF16).astype(F32)
        second_ = (row - first).astype(BF16).astype(F32)
        return first, second_, row - first - second_

    feat_rows = split(feat_row)

    def dots_copy(o):
        to = plane(o // nx, o % nx)
        return remote(
            send_d.at[to], recv_d.at[o], ds_sem, dr_sem, to, par
        )

    for o in [*range(ex_n - 1, 0, -1), 0]:
        b = plane(o // nx, o % nx)
        part = lax.dot_general(
            padded, val_v[b], (((1,), (1,)), ((), ())), preferred_element_type=F32
        )
        extra = jnp.zeros((8, 256), F32)
        for k, row in enumerate((*split(val_sq[b]), *feat_rows)):
            extra = jnp.where(sub == k, row, extra)
        send_d[b] = jnp.concatenate([part[0:rows], extra], axis=0).astype(BF16)
        if o != 0:
            dots_copy(o).start()

    total = send_d[ex].astype(F32)
    every = whole(
        send_d.at[pl.ds(0, ex_n - 1)], recv_d.at[pl.ds(1, ex_n - 1)], ds_sem, dr_sem
    )
    every.wait_recv()
    for o in range(1, ex_n):
        total = total + recv_d[o].astype(F32)
    val_row = total[rows : rows + 1] + total[rows + 1 : rows + 2] + total[rows + 2 : rows + 3]
    feat_row = total[rows + 3 : rows + 4] + total[rows + 4 : rows + 5] + total[rows + 5 : rows + 6]
    feat_sq = jnp.sum(jnp.where(diagonal, feat_row, 0.0), axis=1, keepdims=True)
    factor = float(256 * ex_n) ** 0.5
    out_ref[1] = (
        factor * total[0:rows] * lax.rsqrt(feat_sq + 1e-06) * lax.rsqrt(val_row + 1e-06)
    )

    every.wait_send()
    last.wait_send()

def shards(ny, nx, nz, adapter_inputs, output_gradient, lengths, projection, validation):
    adapter_inputs = jnp.swapaxes(adapter_inputs, 1, 2)
    count, rank, tokens = adapter_inputs.shape
    width = output_gradient.shape[2]
    ex_n, par_n = ny * nx, nz * 2
    groups = count // 8
    vm, dma = pltpu.VMEM, pltpu.SemaphoreType.DMA
    half_z = nz // 2
    x_block, y_block = (half_z, 16, 128), (nx, half_z, 16, 128)
    scratch = [
        pltpu.SMEM(lengths.shape, jnp.int32),
        vm((count, rank, tokens), BF16),
        vm((count, tokens, width), BF16),
        vm(projection.shape, BF16),
        vm((par_n, 256, 256), BF16),
        vm((8 * ex_n * 8, 128), F32),
        vm((groups, ex_n, 16, 512), BF16),
        vm((groups, ex_n, 16, 512), BF16),
        vm((groups * ex_n * 8, 1024), BF16),
        vm((groups * ny, 2, nx, nz, 16, 128), F32),
        vm((groups * ny, nx, nz, 16, 128), F32),
        vm((groups, ny, nx - 1, *x_block), BF16),
        vm((groups, ny, nx - 1, *x_block), BF16),
        vm((groups, ny, *x_block), F32),
        vm((groups, ny - 1, *y_block), BF16),
        vm((groups, ny - 1, *y_block), BF16),
        vm((groups, *y_block), F32),
        vm((2, groups, nx - 1, *x_block), BF16),
        vm((2, groups, nx - 1, *x_block), BF16),
        vm((nz, groups, 16, 128), F32),
        vm((nz, groups, 16, 128), BF16),
        vm((nz - 1, groups, 16, 128), BF16),
        vm((par_n, 8, 256), F32),
        vm((ex_n, 32, 256), BF16),
        vm((ex_n, 32, 256), BF16),
        dma(()),
        dma((groups,)),
        dma((groups,)),
        dma(()),
        dma(()),
        dma((groups,)),
        dma((groups,)),
        dma(()),
        dma((nz,)),
        dma(()),
        dma((nz,)),
        dma(()),
        dma((groups * ny,)),
        dma(()),
        dma((groups, ny)),
        dma(()),
        dma((groups,)),
        dma(()),
        dma((2, groups)),
        dma(()),
        dma(()),
        dma(()),
        dma(()),
    ]
    anywhere = pl.BlockSpec(memory_space=pl.ANY)
    local = pl.BlockSpec(memory_space=pltpu.VMEM)
    out = pl.pallas_call(
        functools.partial(kernel, ny, nx, nz, groups, rank),
        out_shape=jax.ShapeDtypeStruct((2, count, 256), F32),
        in_specs=[anywhere, anywhere, anywhere, anywhere, anywhere],
        out_specs=local,
        scratch_shapes=scratch,
        compiler_params=pltpu.CompilerParams(
            collective_id=0, has_side_effects=True, vmem_limit_bytes=55091 * 1024
        ),
        cost_estimate=pl.CostEstimate(
            flops=4_000_000_000, bytes_accessed=13_000_000, transcendentals=0
        ),
    )(adapter_inputs, output_gradient, lengths, projection, validation)
    return out[0].astype(BF16), out[1]


def solution(mesh):
    ex_n, par_n = mesh.shape["ex"], mesh.shape["par"]
    nx = 1
    while nx * nx < ex_n:
        nx *= 2
    in_specs = (
        P("ex", None, None),
        P("ex", None, "par"),
        P("ex"),
        P(("par", "ex"), None),
        P("par", "ex"),
    )
    out_specs = (P("par", "ex"), P("par", "ex"))
    return jax.shard_map(
        functools.partial(shards, ex_n // nx, nx, par_n // 2),
        mesh=mesh,
        in_specs=in_specs,
        out_specs=out_specs,
        check_vma=False,
    )
```
